32 devices in a mesh: sub: 8 (over y, x, core), grp: 4 (over z).
Axes of the slice: x: 2, y: 2, z: 4, core: 2. Of those that a mesh axis runs over, the one named last changes fastest.
Arguments:
- phi: bfloat16 [64, 400, 2048], P('sub', 'grp'), may hold values from -0.5 to 0.5
- psi: bfloat16 [64, 400, 2048], P('sub', 'grp'), may hold values from -1.25 to 1.25
- k_blocks: bfloat16 [64, 24, 128, 128], P('sub'), may hold values from -0.5 to 0.5
- m_blocks: bfloat16 [64, 24, 128, 128], P('sub'), may hold values from -0.5 to 0.5
- block_row: int32 [64, 24], P('sub'), may hold values from 0 to 15
- block_col: int32 [64, 24], P('sub'), may hold values from 0 to 31
- live: int32 [64], P('sub'), may hold values from 1 to 24, 768 in all
Outputs:
- grid_k: float32 [8, 4, 8, 100, 800], P('sub', 'grp')
- grid_m: float32 [8, 4, 8, 100, 800], P('sub', 'grp')
The draws below stay inside these ranges and needn't reach their ends.
Inputs may be any that keep to these rules, and one draw needn't show every extreme that they name: Slots n >= live[i] are not part of substructure i's pattern; the largest count is 24. `block_row`: several used slots may name the same block position; their terms add. `block_col`: blocks below 16 lie on the left interface, the others on the right one.
All inputs are finite; a program needn't handle non-finite values. No bound on the sum of `live` on one device may be relied on, other than what follows from the above.
Results may differ from the reference program's by a relative error of at most 0.0029.
Values may be sent and summed in bfloat16 or wider, within the bound.
No kernel may reach another device: no remote copies, remote signals or barrier semaphores. Data moves between devices by JAX's collectives and lax.ppermute only.
A program may use at most 256 MiB of HBM per device.

```python
import math
import jax
import jax.numpy as jnp
import numpy as np
from jax import lax

MODES = 400
BLK = 128
NBLK = 16
NNZ = 24
S_DEV = 8
SUBS = 64
IDOF = 2048
RB = 100
N_SUB = 8
N_GRP = 4


def touch_ends(values, rng, low, high):
    index_at = [jax.random.randint(jax.random.fold_in(rng, axis), (), 0, length) for axis, length in enumerate(values.shape)]
    main_axis = values.shape.index(max(values.shape))
    beside = index_at[:main_axis] + [(index_at[main_axis] + 1) % values.shape[main_axis]] + index_at[main_axis + 1:]
    return values.at[tuple(index_at)].set(low).at[tuple(beside)].set(high)


def level_of(stream_key, extent, cuts, low, top_value):
    loudness, own = 1.0, jax.random.fold_in(stream_key, 6)
    for dim, shards_of in cuts:
        heights = jnp.exp(jax.random.uniform(jax.random.fold_in(own, dim), (shards_of,), jnp.float32, low / len(cuts), top_value / len(cuts)))
        loudness = loudness * jnp.repeat(heights, extent[dim] // shards_of).reshape([-1 if axis == dim else 1 for axis in range(len(extent))])
    return loudness


def split_up(count, total, limit, slope):
    weights = [(1 << 20) // math.isqrt(grade ** slope) + 1 for grade in range(2, count + 1)]
    surplus, holding = total - limit - (count - 1), [1] * (count - 1)
    while surplus > 0:
        movable = [i for i in range(count - 1) if holding[i] < limit]
        whole, remaining = sum([weights[i] for i in movable]), surplus
        for i in movable:
            extra = min(limit - holding[i], max(1, remaining * weights[i] // whole), surplus)
            holding[i] = holding[i] + extra
            surplus = surplus - extra
    return np.array([limit] + holding)


def ragged_sizes(stream_key, count, total, reach, lean):
    if count == 2:
        one = jax.random.randint(stream_key, (), max(1, total - reach), min(reach, total - 1) + 1)
        return jnp.stack([one, total - one])
    lengths = jnp.asarray(split_up(count, total, reach, lean), jnp.int32)
    couples = (count - 1) // 2
    giver, receiver = lengths[1:1 + 2 * couples:2], lengths[2:2 + 2 * couples:2]
    margin = jnp.minimum(giver - 1, reach - receiver)
    shifted = jax.random.randint(jax.random.fold_in(stream_key, 1), (couples,), 0, 1 << 20) % (margin + 1)
    lengths = lengths.at[1:1 + 2 * couples:2].set(giver - shifted).at[2:2 + 2 * couples:2].set(receiver + shifted)
    return lengths[jax.random.permutation(jax.random.fold_in(stream_key, 2), count)]


def scatter_about(rng, extent, width, limit, split=(), kind=jnp.bfloat16):
    values = jax.random.normal(rng, extent, jnp.float32) * width
    if len(split) > 0:
        values = level_of(rng, extent, split, -0.22, 0.18) * values
    return jnp.clip(values, min=-limit, max=limit).astype(kind)


def setup_inputs(seed: int = 0) -> dict:
    seeds = jax.random.split(jax.random.key(seed), 8)
    phi = scatter_about(seeds[0], (SUBS, MODES, IDOF), BLK ** -0.5, 0.5, ((0, 8), (1, 4)))
    psi = scatter_about(seeds[1], (SUBS, MODES, IDOF), NNZ ** -0.5, 1.25, ((0, 8), (1, 4)))
    k_blocks = scatter_about(seeds[2], (SUBS, NNZ, BLK, BLK), BLK ** -0.5, 0.5, ((0, 8),))
    m_blocks = scatter_about(seeds[3], (SUBS, NNZ, BLK, BLK), BLK ** -0.5, 0.5, ((0, 8),))
    block_row = touch_ends(jax.random.randint(seeds[4], (SUBS, NNZ), 0, NBLK), jax.random.fold_in(seeds[4], 1), 0, NBLK - 1).astype(jnp.int32)
    block_col = touch_ends(jax.random.randint(seeds[5], (SUBS, NNZ), 0, 2 * NBLK), jax.random.fold_in(seeds[5], 1), 0, (2 * NBLK) - 1).astype(jnp.int32)
    live = ragged_sizes(seeds[6], SUBS, SUBS * NNZ // 2, NNZ, 2).astype(jnp.int32)
    return {"phi": phi, "psi": psi, "k_blocks": k_blocks, "m_blocks": m_blocks, "block_row": block_row, "block_col": block_col, "live": live}


def project(phi_one, blocks, rows, cols, count):
    def add_slot(slot, total):
        start_row = (rows[slot] * BLK).astype(jnp.int32)
        picked = lax.dynamic_slice_in_dim(phi_one, start_row, BLK, 1)
        term = jnp.dot(picked, blocks[slot], preferred_element_type=jnp.float32)
        term = jnp.where(slot < count, term, jnp.zeros_like(term))
        start_col = (cols[slot] * BLK).astype(jnp.int32)
        before = lax.dynamic_slice_in_dim(total, start_col, BLK, 1)
        return lax.dynamic_update_slice_in_dim(total, before + term, start_col, 1)

    empty = jnp.zeros((MODES, 2 * IDOF), jnp.float32)
    return lax.fori_loop(0, NNZ, add_slot, empty)


def arrange(reduced):
    shaped = reduced.reshape(N_SUB, S_DEV, N_GRP, MODES // N_GRP, 2 * MODES)
    shaped = shaped.transpose(0, 2, 1, 3, 4).reshape(N_SUB, N_GRP, N_SUB, RB, 2 * MODES)
    return shaped.transpose(2, 1, 0, 3, 4)


def reference(phi, psi, k_blocks, m_blocks, block_row, block_col, live):
    left_modes = jnp.concatenate([jnp.zeros((1, MODES, IDOF), psi.dtype), psi[:-1]], axis=0)

    def one_sub(items):
        phi_one, left_one, right_one, k_one, m_one, rows, cols, count = items
        results = []
        for blocks in (k_one, m_one):
            coupling = project(phi_one, blocks, rows, cols, count).astype(jnp.bfloat16)
            near = jnp.dot(coupling[:, :IDOF], left_one.T, preferred_element_type=jnp.float32)
            far = jnp.dot(coupling[:, IDOF:], right_one.T, preferred_element_type=jnp.float32)
            results.append(jnp.concatenate([near, far], axis=1))
        return results[0], results[1]

    reduced_k, reduced_m = lax.map(one_sub, (phi, left_modes, psi, k_blocks, m_blocks, block_row, block_col, live))
    return arrange(reduced_k), arrange(reduced_m)
```

```python
import functools

import jax
import jax.numpy as jnp
from jax import lax
from jax.experimental import pallas as pl
from jax.experimental.pallas import tpu as pltpu
from jax.sharding import PartitionSpec as P

EDGE = 128
ROWS = 112
BITE = 4
MIB = 1 << 20


def up_to(limit, body):
    lax.fori_loop(0, limit, lambda n, _: (body(n), 0)[1], 0)


def lanes(block, count=1):
    return pl.ds(pl.multiple_of(block * EDGE, EDGE), count * EDGE)


class Meta:
    def __init__(self, count, slots, blocks_per):
        self.count, self.slots, self.blocks_per = count, slots, blocks_per
        self.keys = (count + 1) * blocks_per
        self.order = 0
        self.start = self.keys
        self.live = self.start + count + 2
        self.row = self.live + count
        self.col = self.row + count * slots


def listed(meta_at, block_row, block_col, live):
    count, slots = block_row.shape
    keys = meta_at.keys
    used = jnp.arange(slots, dtype=jnp.int32)[None, :] < live[:, None]
    key = block_col + meta_at.blocks_per * jnp.arange(count, dtype=jnp.int32)[:, None]
    every = jnp.arange(keys, dtype=jnp.int32)
    need = jnp.any((key[:, :, None] == every) & used[:, :, None], axis=(0, 1))
    before = jnp.sum(jnp.where(need[None, :] & (every[None, :] < every[:, None]), 1, 0), axis=1)
    hit = need[None, :] & (before[None, :] == every[:, None])
    order = jnp.sum(jnp.where(hit, every[None, :], 0), axis=1)
    edges = meta_at.blocks_per * jnp.arange(count + 2, dtype=jnp.int32)
    start = jnp.sum(jnp.where(need[None, :] & (every[None, :] < edges[:, None]), 1, 0), axis=1)
    meta = jnp.concatenate(
        [order, start, live, block_row.reshape(-1), block_col.reshape(-1)]
    ).astype(jnp.int32)
    return meta, start[count + 1]


def pack_kernel(at, room, meta, psi, border, out):
    def one(c):
        key = meta[at.order + c]
        side, block = key // at.blocks_per, key % at.blocks_per

        @pl.when(side == 0)
        def _():
            out[:, lanes(c)] = border[:, lanes(block)]

        @pl.when(side > 0)
        def _():
            out[:, lanes(c)] = psi[side - 1, :, lanes(block)]

    up_to(room, one)


def pack(at, room, meta, psi, border):
    return pl.pallas_call(
        functools.partial(pack_kernel, at, room),
        out_shape=jax.ShapeDtypeStruct((psi.shape[1], room * EDGE), psi.dtype),
        in_specs=[
            pl.BlockSpec(memory_space=pltpu.SMEM),
            pl.BlockSpec(memory_space=pltpu.VMEM),
            pl.BlockSpec(memory_space=pltpu.VMEM),
        ],
        out_specs=pl.BlockSpec(memory_space=pltpu.VMEM),
        compiler_params=pltpu.CompilerParams(vmem_limit_bytes=24 * MIB),
        cost_estimate=pl.CostEstimate(flops=0, bytes_accessed=8 * MIB, transcendentals=0),
    )(meta, psi, border)


def coupling_kernel(at, room, meta, phi, k_blocks, m_blocks, out, total):
    i = pl.program_id(0)
    modes = phi.shape[1]
    here, middle, end = (meta[at.start + i + n] for n in range(3))
    first = at.blocks_per * i

    def clear(n):
        total[meta[at.order + here + n] - first] = jnp.zeros(total.shape[1:], total.dtype)

    up_to(end - here, clear)

    def add_slot(n):
        row, col = (meta[base + i * at.slots + n] for base in (at.row, at.col))
        picked = phi[0, :, lanes(row)]
        total[col, :, :EDGE] += jnp.dot(picked, k_blocks[0, n], preferred_element_type=jnp.float32)
        total[col, :, EDGE:] += jnp.dot(picked, m_blocks[0, n], preferred_element_type=jnp.float32)

    up_to(meta[at.live + i], add_slot)

    def put(flavour, c):
        done = total[meta[at.order + c] - first].astype(out.dtype)
        out[flavour * ROWS : flavour * ROWS + modes, lanes(c)] = done[:, :EDGE]
        out[(flavour + 1) * ROWS : (flavour + 1) * ROWS + modes, lanes(c)] = done[:, EDGE:]

    def blank(top, c):
        out[top : top + 2 * ROWS, lanes(c)] = jnp.zeros((2 * ROWS, EDGE), out.dtype)

    up_to(middle - here, lambda n: put(2, here + n))
    up_to(end - middle, lambda n: put(0, middle + n))

    @pl.when(i == 0)
    def _():
        up_to(middle, lambda n: blank(0, n))

    @pl.when(i == at.count - 1)
    def _():
        up_to(room - middle, lambda n: blank(2 * ROWS, middle + n))
        up_to(room - end, lambda n: blank(0, end + n))


def couple(at, room, meta, phi, k_blocks, m_blocks):
    count, modes, width = phi.shape
    slots = k_blocks.shape[1]
    return pl.pallas_call(
        functools.partial(coupling_kernel, at, room),
        out_shape=jax.ShapeDtypeStruct((4 * ROWS, room * EDGE), phi.dtype),
        grid_spec=pltpu.PrefetchScalarGridSpec(
            num_scalar_prefetch=1,
            grid=(count,),
            in_specs=[
                pl.BlockSpec((1, modes, width), lambda i, meta: (i, 0, 0)),
                pl.BlockSpec((1, slots, EDGE, EDGE), lambda i, meta: (i, 0, 0, 0)),
                pl.BlockSpec((1, slots, EDGE, EDGE), lambda i, meta: (i, 0, 0, 0)),
            ],
            out_specs=pl.BlockSpec((4 * ROWS, room * EDGE), lambda i, meta: (0, 0)),
            scratch_shapes=[pltpu.VMEM((2 * at.blocks_per, modes, 2 * EDGE), jnp.float32)],
        ),
        compiler_params=pltpu.CompilerParams(vmem_limit_bytes=52 * MIB),
        cost_estimate=pl.CostEstimate(
            flops=20_000_000_000, bytes_accessed=32 * MIB, transcendentals=0
        ),
    )(meta, phi, k_blocks, m_blocks)


def project_kernel(at, room, sets, meta, coupling, *refs):
    shards = refs[: sum(sets)]
    outs = refs[sum(sets) : sum(sets) + len(sets)]
    totals = refs[sum(sets) + len(sets) :]
    modes = shards[0].shape[0]
    groups, taken = [], 0
    for size in sets:
        groups.append(shards[taken : taken + size])
        taken += size
    for side in range(at.count + 1):
        here, end = meta[at.start + side], meta[at.start + side + 1]
        for total in totals:
            total[...] = jnp.zeros(total.shape, total.dtype)

        def bite(n):
            want = here + n * BITE
            first = jnp.minimum(want, room - BITE)
            lane = lax.broadcasted_iota(jnp.int32, (modes, BITE * EDGE), 1) + first * EDGE
            inside = (lane >= want * EDGE) & (lane < end * EDGE)
            left = coupling[:, lanes(first, BITE)]
            for group, total in zip(groups, totals):
                right = group[0][:, lanes(first, BITE)]
                for other in group[1:]:
                    right = right + other[:, lanes(first, BITE)]
                right = jnp.where(inside, right, jnp.zeros_like(right))
                total[...] += lax.dot_general(
                    left, right, (((1,), (1,)), ((), ())), preferred_element_type=jnp.float32
                )

        up_to((end - here + BITE - 1) // BITE, bite)
        for total, out in zip(totals, outs):
            for flavour, (sub, part) in enumerate(
                ((side - 1, 1), (side - 1, 3), (side, 0), (side, 2))
            ):
                if 0 <= sub < at.count:
                    top = flavour * ROWS
                    out[sub, part] = total[top : top + modes, :].astype(out.dtype)


def project(at, room, meta, coupling, groups):
    modes = groups[0][0].shape[0]
    flat = [shard for group in groups for shard in group]
    shape = (at.count, 4, modes, modes)
    return pl.pallas_call(
        functools.partial(project_kernel, at, room, tuple(len(group) for group in groups)),
        out_shape=[jax.ShapeDtypeStruct(shape, coupling.dtype)] * len(groups),
        in_specs=[pl.BlockSpec(memory_space=pltpu.SMEM)]
        + [pl.BlockSpec(memory_space=pltpu.VMEM)] * (1 + len(flat)),
        out_specs=[pl.BlockSpec(memory_space=pltpu.VMEM)] * len(groups),
        scratch_shapes=[pltpu.VMEM((4 * ROWS, modes), jnp.float32)] * len(groups),
        compiler_params=pltpu.CompilerParams(vmem_limit_bytes=48 * MIB),
        cost_estimate=pl.CostEstimate(
            flops=8_000_000_000 * len(groups), bytes_accessed=16 * MIB, transcendentals=0
        ),
    )(meta, coupling, *flat)


def assemble_kernel(place, own, left, right, second, third, grid_k, grid_m):
    modes = own.shape[-1]
    plans = (
        {0: own, 1: right, 2: second, 3: third},
        {0: left, 1: own, 2: right, 3: second},
        {0: second, 1: left, 2: own, 3: right},
        {0: third, 1: second, 2: left, 3: own},
    )
    for z, plan in enumerate(plans):

        @pl.when(place[0] == z)
        def _(plan=plan):
            for grid, low in ((grid_k, 0), (grid_m, 2)):
                wide = [plan[h][0, low + n] for n in range(2) for h in range(4)]
                grid[0] = jnp.concatenate([one.astype(jnp.float32) for one in wide], axis=1)


def assemble(place, parts):
    owners, _, rows, modes = parts[0].shape
    out = jax.ShapeDtypeStruct((owners, rows, 8 * modes), jnp.float32)
    return pl.pallas_call(
        assemble_kernel,
        out_shape=[out, out],
        grid_spec=pltpu.PrefetchScalarGridSpec(
            num_scalar_prefetch=1,
            grid=(owners,),
            in_specs=[pl.BlockSpec((1, 4, rows, modes), lambda d, place: (d, 0, 0, 0))] * 5,
            out_specs=[pl.BlockSpec((1, rows, 8 * modes), lambda d, place: (d, 0, 0))] * 2,
        ),
        cost_estimate=pl.CostEstimate(flops=0, bytes_accessed=10 * MIB, transcendentals=0),
    )(place, *parts)


def moved(shard, axis, by, sources=None):
    length = lax.axis_size(axis)
    sources = range(length) if sources is None else sources
    pairs = [(i, i + by) for i in sources if 0 <= i + by < length]
    return lax.ppermute(shard, axis, pairs)


def to_owners(part):
    owners = lax.axis_size("sub")
    count, flavours, modes, cols = part.shape
    cut = owners // count
    part = part.reshape(count, flavours, cut, modes // cut, cols).transpose(0, 2, 1, 3, 4)
    part = part.reshape(owners, flavours, modes // cut, cols)
    return lax.all_to_all(part, "sub", split_axis=0, concat_axis=0, tiled=True)


def with_room(at, room, meta, phi, psi, border, k_blocks, m_blocks):
    packed = pack(at, room, meta, psi, border)
    left1, right1 = moved(packed, "grp", 1), moved(packed, "grp", -1)
    coupling = couple(at, room, meta, phi, k_blocks, m_blocks)
    (own,) = project(at, room, meta, coupling, [(packed,)])
    own = to_owners(own)
    left2, right2 = moved(left1, "grp", 1), moved(right1, "grp", -1)
    left, right = project(at, room, meta, coupling, [(left1,), (right1,)])
    left, right = to_owners(left), to_owners(right)
    left3, right3 = moved(left2, "grp", 1), moved(right2, "grp", -1)
    (second,) = project(at, room, meta, coupling, [(left2, right2)])
    second = to_owners(second)
    (third,) = project(at, room, meta, coupling, [(left3, right3)])
    third = to_owners(third)
    place = lax.axis_index("grp").astype(jnp.int32)[None]
    return assemble(place, (own, left, right, second, third))


def per_device(phi, psi, k_blocks, m_blocks, block_row, block_col, live):
    count, _, width = phi.shape
    at = Meta(count, k_blocks.shape[1], width // EDGE)
    border = moved(psi[count - 1], "sub", 1)
    meta, needed = listed(at, block_row, block_col, live)
    most = lax.pmax(needed, "sub")
    rooms = [room for room in (64, 72, 80, 88, 96, 112) if room < at.keys] + [at.keys]
    pick = jnp.sum((most > jnp.asarray(rooms[:-1], jnp.int32)).astype(jnp.int32))
    branches = [functools.partial(with_room, at, room) for room in rooms]
    grid_k, grid_m = lax.switch(pick, branches, meta, phi, psi, border, k_blocks, m_blocks)
    return (grid_k[None, None], grid_m[None, None])


def solution(mesh):
    placed = (
        P("sub", "grp", None),
        P("sub", "grp", None),
        P("sub", None, None, None),
        P("sub", None, None, None),
        P("sub", None),
        P("sub", None),
        P("sub"),
    )
    return jax.shard_map(
        per_device,
        mesh=mesh,
        in_specs=placed,
        out_specs=(P("sub", "grp", None, None, None), P("sub", "grp", None, None, None)),
        check_vma=False,
    )
```

```python
import functools

import jax
import jax.numpy as jnp
from jax import lax
from jax.experimental import pallas as pl
from jax.experimental.pallas import tpu as pltpu
from jax.sharding import PartitionSpec as P

EDGE = 128
ROWS = 112
SLOTS = 4
BITE = 4
ROOM = 88
MORE = 16
MIB = 1 << 20
LIGHT = pl.CostEstimate(flops=1, bytes_accessed=1, transcendentals=0)


def up_to(limit, body, unroll=1):
    lax.fori_loop(0, limit, lambda n, _: (body(n), 0)[1], 0, unroll=unroll)


def lanes(block, count=1):
    return pl.ds(pl.multiple_of(block * EDGE, EDGE), count * EDGE)


class Meta:
    def __init__(self, count, slots, blocks_per):
        self.count, self.slots, self.blocks_per = count, slots, blocks_per
        self.keys = (count + 1) * blocks_per
        self.order = 0
        self.start = self.keys + ROOM + MORE
        self.size = self.start + count + 2


def list_kernel(at, live, col, meta, flags):
    def clear(n):
        flags[n] = 0

    up_to(at.keys, clear, unroll=16)
    for i in range(at.count):

        def mark(n, i=i):
            flags[col[i, n] + i * at.blocks_per] = 1

        up_to(live[i], mark)

    def place(key, taken):
        meta[at.order + taken] = key
        return taken + flags[key]

    taken = 0
    for side in range(at.count + 1):
        meta[at.start + side] = taken
        taken = lax.fori_loop(
            side * at.blocks_per, (side + 1) * at.blocks_per, place, taken, unroll=at.blocks_per
        )
    meta[at.start + at.count + 1] = taken

    def fill(n):
        meta[at.order + n] = at.blocks_per

    lax.fori_loop(taken, at.start, lambda n, _: (fill(n), 0)[1], 0)


def listed(at, block_col, live):
    return pl.pallas_call(
        functools.partial(list_kernel, at),
        out_shape=jax.ShapeDtypeStruct((at.size,), jnp.int32),
        in_specs=[pl.BlockSpec(memory_space=pltpu.SMEM)] * 2,
        out_specs=pl.BlockSpec(memory_space=pltpu.SMEM),
        scratch_shapes=[pltpu.SMEM((at.keys,), jnp.int32)],
    )(live, block_col)


def pack_kernel(at, first, room, meta, psi, border, out):
    def one(c):
        key = meta[at.order + first + c]
        side, block = key // at.blocks_per, key % at.blocks_per

        @pl.when(side == 0)
        def _():
            out[:, lanes(c)] = border[:, lanes(block)]

        @pl.when(side > 0)
        def _():
            out[:, lanes(c)] = psi[side - 1, :, lanes(block)]

    up_to(room, one)


def pack(at, first, room, meta, psi, border):
    return pl.pallas_call(
        functools.partial(pack_kernel, at, first, room),
        out_shape=jax.ShapeDtypeStruct((psi.shape[1], room * EDGE), psi.dtype),
        in_specs=[
            pl.BlockSpec(memory_space=pltpu.SMEM),
            pl.BlockSpec(memory_space=pltpu.VMEM),
            pl.BlockSpec(memory_space=pltpu.VMEM),
        ],
        out_specs=pl.BlockSpec(memory_space=pltpu.VMEM),
        compiler_params=pltpu.CompilerParams(vmem_limit_bytes=8 * MIB),
        cost_estimate=LIGHT,
    )(meta, psi, border)


def coupling_kernel(at, room, meta, live, row, col, phi, k_blocks, m_blocks, out, total):
    i = pl.program_id(0)
    modes = phi.shape[1]
    here, middle, end = (meta[at.start + i + n] for n in range(3))
    first = at.blocks_per * i

    def clear(n):
        total[meta[at.order + here + n] - first] = jnp.zeros(total.shape[1:], total.dtype)

    up_to(end - here, clear)

    def add_slots(step):
        terms = []
        for n in range(SLOTS):
            slot = jnp.minimum(step * SLOTS + n, at.slots - 1)
            picked = phi[0, :, lanes(row[i, slot])]
            both = jnp.concatenate([k_blocks[0, slot], m_blocks[0, slot]], axis=1)
            to = jnp.where(step * SLOTS + n < live[i], col[i, slot], 2 * at.blocks_per)
            terms.append((to, jnp.dot(picked, both, preferred_element_type=jnp.float32)))
        for to, term in terms:
            total[to] += term

    up_to((live[i] + SLOTS - 1) // SLOTS, add_slots)

    def put(flavour, c):
        done = total[meta[at.order + c] - first].astype(out.dtype)
        out[flavour * ROWS : flavour * ROWS + modes, lanes(c)] = done[:, :EDGE]
        out[(flavour + 1) * ROWS : (flavour + 1) * ROWS + modes, lanes(c)] = done[:, EDGE:]

    def blank(top, c):
        out[top : top + 2 * ROWS, lanes(c)] = jnp.zeros((2 * ROWS, EDGE), out.dtype)

    up_to(middle - here, lambda n: put(2, here + n))
    up_to(end - middle, lambda n: put(0, middle + n))

    @pl.when(i == 0)
    def _():
        up_to(middle, lambda n: blank(0, n))

    @pl.when(i == at.count - 1)
    def _():
        up_to(room - middle, lambda n: blank(2 * ROWS, middle + n))
        up_to(room - end, lambda n: blank(0, end + n))


def couple(at, room, meta, live, row, col, phi, k_blocks, m_blocks):
    count, modes, width = phi.shape
    slots = k_blocks.shape[1]
    return pl.pallas_call(
        functools.partial(coupling_kernel, at, room),
        out_shape=jax.ShapeDtypeStruct((4 * ROWS, room * EDGE), phi.dtype),
        grid_spec=pltpu.PrefetchScalarGridSpec(
            num_scalar_prefetch=4,
            grid=(count,),
            in_specs=[
                pl.BlockSpec((1, modes, width), lambda i, *_: (i, 0, 0)),
                pl.BlockSpec((1, slots, EDGE, EDGE), lambda i, *_: (i, 0, 0, 0)),
                pl.BlockSpec((1, slots, EDGE, EDGE), lambda i, *_: (i, 0, 0, 0)),
            ],
            out_specs=pl.BlockSpec(
                (4 * ROWS, room * EDGE), lambda i, *_: (0, 0), pipeline_mode=pl.Buffered(1)
            ),
            scratch_shapes=[pltpu.VMEM((2 * at.blocks_per + 1, modes, 2 * EDGE), jnp.float32)],
        ),
        compiler_params=pltpu.CompilerParams(vmem_limit_bytes=56 * MIB),
        cost_estimate=LIGHT,
    )(meta, live, row, col, phi, k_blocks, m_blocks)


def project_kernel(at, cuts, sets, meta, coupling, *refs):
    pieces, many = len(cuts) - 1, sum(sets)
    shards, refs = refs[: many * pieces], refs[many * pieces :]
    out, held, shard, right, total, held_done, shard_done = refs
    modes = shard.shape[1]
    middles = [(low + high) // 2 for low, high in zip(cuts, cuts[1:])]
    bounds = sorted((*cuts, *middles))
    parts = list(zip(bounds, bounds[1:]))
    coming = []
    for n, (low, high) in enumerate(parts):
        to, here = pl.ds(low * EDGE, (high - low) * EDGE), []
        if n % 2 == 0:
            piece = n // 2
            whole = pl.ds(cuts[piece] * EDGE, (cuts[piece + 1] - cuts[piece]) * EDGE)
            for k in range(many):
                one = k * pieces + piece
                here.append(
                    pltpu.make_async_copy(shards[one], shard.at[k, :, whole], shard_done.at[one])
                )
        here.append(pltpu.make_async_copy(coupling.at[:, to], held.at[:, to], held_done.at[n]))
        for copy in here:
            copy.start()
        coming.append(here)
    groups, taken = [], 0
    for size in sets:
        groups.append(range(taken, taken + size))
        taken += size
    right[...] = jnp.zeros(right.shape, right.dtype)
    total[...] = jnp.zeros(total.shape, total.dtype)
    for (low, high), here in zip(parts, coming):
        for copy in here:
            copy.wait()

        def on_side(side, low=low, high=high):
            begin = jnp.maximum(meta[at.start + side], low)
            end = jnp.minimum(meta[at.start + side + 1], high)

            def bite(n):
                want = begin + n * BITE
                first = jnp.minimum(want, high - BITE)
                lane = lax.broadcasted_iota(jnp.int32, (modes, BITE * EDGE), 1) + first * EDGE
                inside = (lane >= want * EDGE) & (lane < end * EDGE)
                for g, group in enumerate(groups):
                    part = shard[group[0], :, lanes(first, BITE)]
                    for other in group[1:]:
                        part = part + shard[other, :, lanes(first, BITE)]
                    part = jnp.where(inside, part, jnp.zeros_like(part))
                    right[g * EDGE : g * EDGE + modes, :] = part
                total[side] += lax.dot_general(
                    held[:, lanes(first, BITE)],
                    right[...],
                    (((1,), (1,)), ((), ())),
                    preferred_element_type=jnp.float32,
                )

            up_to(jnp.maximum(end - begin + BITE - 1, 0) // BITE, bite)

        up_to(at.count + 1, on_side)
    for side in range(at.count + 1):
        for g in range(len(groups)):
            for flavour, (sub, part) in enumerate(
                ((side - 1, 1), (side - 1, 3), (side, 0), (side, 2))
            ):
                if 0 <= sub < at.count:
                    top, to = flavour * ROWS, (g * 4 + part) * modes
                    one = total[side, top : top + modes, g * EDGE : g * EDGE + modes]
                    out[sub, :, to : to + modes] = one.astype(out.dtype)


def project(at, cuts, meta, coupling, groups):
    modes = groups[0][0][0].shape[0]
    flat = [piece for group in groups for shard in group for piece in shard]
    sets = tuple(len(group) for group in groups)
    n = len(groups)
    wide = -(-n * 4 * modes // EDGE) * EDGE
    return pl.pallas_call(
        functools.partial(project_kernel, at, cuts, sets),
        out_shape=jax.ShapeDtypeStruct((at.count, modes, wide), coupling.dtype),
        in_specs=[pl.BlockSpec(memory_space=pltpu.SMEM)]
        + [pl.BlockSpec(memory_space=pltpu.HBM)] * (1 + len(flat)),
        out_specs=pl.BlockSpec(memory_space=pltpu.VMEM),
        scratch_shapes=[
            pltpu.VMEM(coupling.shape, coupling.dtype),
            pltpu.VMEM((sum(sets), modes, coupling.shape[1]), coupling.dtype),
            pltpu.VMEM((n * EDGE, BITE * EDGE), coupling.dtype),
            pltpu.VMEM((at.count + 1, 4 * ROWS, n * EDGE), jnp.float32),
            pltpu.SemaphoreType.DMA((2 * (len(cuts) - 1),)),
            pltpu.SemaphoreType.DMA((len(flat),)),
        ],
        compiler_params=pltpu.CompilerParams(vmem_limit_bytes=56 * MIB),
        cost_estimate=LIGHT,
    )(meta, coupling, *flat)


def assemble_kernel(modes, place, near, late, *refs):
    befores, (grid_k, grid_m, wide) = refs[:-3], refs[-3:]
    own, left, right = ((near, g) for g in range(3))
    second, third = ((late, g) for g in range(2))
    plans = (
        (own, right, second, third),
        (left, own, right, second),
        (second, left, own, right),
        (third, second, left, own),
    )
    for which, grid in enumerate((grid_k, grid_m)):
        for z, plan in enumerate(plans):

            @pl.when(place[0] == z)
            def _(plan=plan, which=which):
                for far in range(2):
                    for h, (part, g) in enumerate(plan):
                        take = (g * 4 + 2 * which + far) * modes
                        at = (4 * far + h) * modes
                        wide[:, :, at : at + modes] = part[:, :, take : take + modes].astype(
                            jnp.float32
                        )

        new = jnp.transpose(wide[...], (1, 0, 2))
        grid[...] = new + befores[which][...] if befores else new


def assemble(place, parts, modes, before=None):
    owners, rows, _ = parts[0].shape
    out = jax.ShapeDtypeStruct((rows, owners, 8 * modes), jnp.float32)
    group = min(owners, 8)
    block = pl.BlockSpec((rows, group, 8 * modes), lambda d, place: (0, d, 0))
    befores = [] if before is None else list(before)
    return pl.pallas_call(
        functools.partial(assemble_kernel, modes),
        out_shape=[out, out],
        grid_spec=pltpu.PrefetchScalarGridSpec(
            num_scalar_prefetch=1,
            grid=(owners // group,),
            in_specs=[
                pl.BlockSpec((group, *part.shape[1:]), lambda d, place: (d, 0, 0)) for part in parts
            ]
            + [block] * len(befores),
            out_specs=[block] * 2,
            scratch_shapes=[pltpu.VMEM((group, rows, 8 * modes), jnp.float32)],
        ),
        input_output_aliases={1 + len(parts) + n: n for n in range(len(befores))},
        compiler_params=pltpu.CompilerParams(vmem_limit_bytes=56 * MIB),
        cost_estimate=LIGHT,
    )(place, *parts, *befores)


def moved(shard, axis, by):
    length = lax.axis_size(axis)
    pairs = [(i, i + by) for i in range(length) if 0 <= i + by < length]
    return lax.ppermute(shard, axis, pairs)


def to_owners(part):
    count, modes, cols = part.shape
    owners = lax.axis_size("sub")
    part = part.reshape(owners, count * modes // owners, cols)
    return lax.all_to_all(part, "sub", split_axis=0, concat_axis=0, tiled=True)


def one_round(at, room, meta, ints, phi, psi, border, k_blocks, m_blocks, beside, before=None):
    modes = phi.shape[1]
    cuts = (0, room // 2, room)
    hold = lax.optimization_barrier

    def both_ways(left, right):
        return moved(left, "grp", 1), moved(right, "grp", -1)

    own_a = pack(at, cuts[0], cuts[1] - cuts[0], meta, psi, border)
    one_a = both_ways(own_a, own_a)
    meta, own_a = hold((meta, own_a))
    own_b = pack(at, cuts[1], cuts[2] - cuts[1], meta, psi, border)
    one_b = both_ways(own_b, own_b)
    one_a, beside, phi = hold((one_a, beside, phi))
    two_a = both_ways(*one_a)
    coupling = couple(at, room, meta, *ints, phi, k_blocks, m_blocks)
    one_b, coupling = hold((one_b, coupling))
    two_b = both_ways(*one_b)
    near = [((own_a, own_b),), ((one_a[0], one_b[0]),), ((one_a[1], one_b[1]),)]
    near = project(at, cuts, meta, coupling, near)
    two_a, near = hold((two_a, near))
    three_a = both_ways(*two_a)
    near = to_owners(near)
    three_a, two_b = hold((three_a, two_b))
    three_b = both_ways(*two_b)
    three_b, near = hold((three_b, near))
    late = [tuple(zip(a, b)) for a, b in ((two_a, two_b), (three_a, three_b))]
    late = to_owners(project(at, cuts, meta, coupling, late))
    place = lax.axis_index("grp").astype(jnp.int32)[None]
    return assemble(place, (near, late), modes, before), beside


def shifted(at, meta, by, room):
    kept = jnp.concatenate([meta[: at.start], jnp.full((at.start,), at.blocks_per, jnp.int32)])
    order = lax.dynamic_slice_in_dim(kept, by, at.start, 0)
    return jnp.concatenate([order, jnp.clip(meta[at.start :] - by, 0, room)])


def per_device(phi, psi, k_blocks, m_blocks, block_row, block_col, live):
    count, modes, width = phi.shape
    at = Meta(count, k_blocks.shape[1], width // EDGE)
    border = moved(psi[count - 1], "sub", 1)
    whole = listed(at, block_col, live)
    ints = (live, block_row, block_col)
    most = lax.pmax(whole[at.start + count + 1], "sub")
    meta = jnp.concatenate([whole[: at.start], jnp.minimum(whole[at.start :], ROOM)])
    grids, most = one_round(at, ROOM, meta, ints, phi, psi, border, k_blocks, m_blocks, most)

    def turned(whole):
        return whole.transpose(1, 0, 2)

    def go_on(state):
        return state[0] < most

    def further(state):
        done, phi, psi, before = state[0], state[1], state[2], state[3:]
        phi, psi = (turned(one) for one in lax.optimization_barrier((phi, psi)))
        meta = shifted(at, whole, done, MORE)
        after, _ = one_round(
            at, MORE, meta, ints, phi, psi, border, k_blocks, m_blocks, done, before
        )
        return (done + MORE, *state[1:3], *after)

    state = lax.while_loop(go_on, further, (jnp.int32(ROOM), turned(phi), turned(psi), *grids))
    return tuple(turned(grid)[None, None] for grid in state[3:])


def solution(mesh):
    placed = (
        P("sub", "grp", None),
        P("sub", "grp", None),
        P("sub", None, None, None),
        P("sub", None, None, None),
        P("sub", None),
        P("sub", None),
        P("sub"),
    )
    return jax.shard_map(
        per_device,
        mesh=mesh,
        in_specs=placed,
        out_specs=(P("sub", "grp", None, None, None), P("sub", "grp", None, None, None)),
        check_vma=False,
    )
```

```python
import functools

import jax
import jax.numpy as jnp
from jax import lax
from jax.experimental import pallas as pl
from jax.experimental.pallas import tpu as pltpu
from jax.sharding import PartitionSpec as P

EDGE = 128
ROWS = 112
SLOTS = 4
BITE = 4
ROOM = 88
PHI_ROOM = 88
MORE = 16
TALL = 32
MIB = 1 << 20
LIGHT = pl.CostEstimate(flops=1, bytes_accessed=1, transcendentals=0)
HEAVY = pl.CostEstimate(flops=25_000_000_000, bytes_accessed=1, transcendentals=0)


def up_to(limit, body, unroll=1):
    lax.fori_loop(0, limit, lambda n, _: (body(n), 0)[1], 0, unroll=unroll)


def lanes(block, count=1):
    return pl.ds(pl.multiple_of(block * EDGE, EDGE), count * EDGE)


class Meta:
    def __init__(self, count, slots, blocks_per):
        self.count, self.slots, self.blocks_per = count, slots, blocks_per
        self.keys = (count + 1) * blocks_per
        self.order = 0
        self.start = self.keys + max(ROOM + MORE, 2 * PHI_ROOM)
        self.size = self.start + count + 2


def list_kernel(at, shift, live, block, meta, *refs):
    (*places, flags) = refs

    def clear(n):
        flags[n] = 0

    up_to(at.keys, clear, unroll=16)
    for i in range(at.count):

        def mark(n, i=i):
            flags[block[i, n] + (i + shift) * at.blocks_per] = 1

        up_to(live[i], mark)

    def place(key, taken):
        needed = flags[key]
        meta[at.order + taken] = key
        flags[key] = taken
        return taken + needed

    taken = 0
    for side in range(at.count + 1):
        meta[at.start + side] = taken
        taken = lax.fori_loop(
            side * at.blocks_per, (side + 1) * at.blocks_per, place, taken, unroll=at.blocks_per
        )
    meta[at.start + at.count + 1] = taken

    for found in places:
        for i in range(at.count):

            def find(n, i=i, found=found):
                found[i, n] = flags[block[i, n] + (i + shift) * at.blocks_per]

            up_to(live[i], find)


def listed(at, shift, block, live, with_places=False):
    out = [jax.ShapeDtypeStruct((at.size,), jnp.int32)]
    if with_places:
        out.append(jax.ShapeDtypeStruct(block.shape, jnp.int32))
    return pl.pallas_call(
        functools.partial(list_kernel, at, shift),
        out_shape=out,
        in_specs=[pl.BlockSpec(memory_space=pltpu.SMEM)] * 2,
        out_specs=[pl.BlockSpec(memory_space=pltpu.SMEM)] * len(out),
        scratch_shapes=[pltpu.SMEM((at.keys,), jnp.int32)],
        cost_estimate=LIGHT,
    )(live, block)


def pack_kernel(at, first, room, meta, *refs):
    borders, psi, out = refs[:-2], refs[-2], refs[-1]

    def one(c):
        key = jnp.where(first + c < meta[at.start + at.count + 1], meta[at.order + first + c], at.blocks_per)
        side, block = key // at.blocks_per, key % at.blocks_per
        for border in borders:

            @pl.when(side == 0)
            def _(border=border):
                out[:, lanes(c)] = border[:, lanes(block)]

        @pl.when(side > 0)
        def _():
            out[:, lanes(c)] = psi[side - 1, :, lanes(block)]

    up_to(room, one)


def pack(at, first, room, meta, psi, *borders):
    return pl.pallas_call(
        functools.partial(pack_kernel, at, first, room),
        out_shape=jax.ShapeDtypeStruct((psi.shape[1], room * EDGE), psi.dtype),
        in_specs=[pl.BlockSpec(memory_space=pltpu.SMEM)]
        + [pl.BlockSpec(memory_space=pltpu.VMEM)] * (1 + len(borders)),
        out_specs=pl.BlockSpec(memory_space=pltpu.VMEM),
        compiler_params=pltpu.CompilerParams(vmem_limit_bytes=8 * MIB),
        cost_estimate=LIGHT,
    )(meta, *borders, psi)


def coupling_kernel(at, room, many, meta, live, row, col, *refs):
    phis, (k_blocks, m_blocks, out, total) = refs[:many], refs[many:]
    i = pl.program_id(0)
    couple_one(at, room, i, meta, live, row, col, phis, k_blocks, m_blocks, out, total)


def couple_one(at, room, i, meta, live, row, col, phis, k_blocks, m_blocks, out, total):
    modes, blocks = phis[0].shape[1], phis[0].shape[2] // EDGE
    here, middle, end = (meta[at.start + i + n] for n in range(3))
    first = at.blocks_per * i

    def clear(n):
        total[meta[at.order + here + n] - first] = jnp.zeros(total.shape[1:], total.dtype)

    up_to(end - here, clear)

    def add_slots(step):
        terms = []
        for n in range(SLOTS):
            slot = jnp.minimum(step * SLOTS + n, at.slots - 1)
            where = row[i, slot]
            here = (step * SLOTS + n < live[i]) & (where >= 0) & (where < blocks)
            which = lanes(jnp.clip(where, 0, blocks - 1))
            picked = sum([phi[0, :, which] for phi in phis[1:]], phis[0][0, :, which])
            both = jnp.concatenate([k_blocks[0, slot], m_blocks[0, slot]], axis=1)
            to = jnp.where(here, col[i, slot], 2 * at.blocks_per)
            terms.append((to, jnp.dot(picked, both, preferred_element_type=jnp.float32)))
        for to, term in terms:
            total[to] += term

    up_to((live[i] + SLOTS - 1) // SLOTS, add_slots)

    def put(flavour, c):
        done = total[meta[at.order + c] - first].astype(out.dtype)
        out[flavour * ROWS : flavour * ROWS + modes, lanes(c)] = done[:, :EDGE]
        out[(flavour + 1) * ROWS : (flavour + 1) * ROWS + modes, lanes(c)] = done[:, EDGE:]

    def blank(top, c):
        out[top : top + 2 * ROWS, lanes(c)] = jnp.zeros((2 * ROWS, EDGE), out.dtype)

    up_to(middle - here, lambda n: put(2, here + n))
    up_to(end - middle, lambda n: put(0, middle + n))

    @pl.when(i == 0)
    def _():
        up_to(middle, lambda n: blank(0, n))

    @pl.when(i == at.count - 1)
    def _():
        up_to(room - middle, lambda n: blank(2 * ROWS, middle + n))
        up_to(room - end, lambda n: blank(0, end + n))


def couple(at, room, meta, live, row, col, phis, k_blocks, m_blocks, cost=LIGHT):
    _, modes, width = phis[0].shape
    count, slots = k_blocks.shape[:2]
    return pl.pallas_call(
        functools.partial(coupling_kernel, at, room, len(phis)),
        out_shape=jax.ShapeDtypeStruct((4 * ROWS, room * EDGE), phis[0].dtype),
        grid_spec=pltpu.PrefetchScalarGridSpec(
            num_scalar_prefetch=4,
            grid=(count,),
            in_specs=[
                pl.BlockSpec(
                    (1, modes, width), lambda i, *_, phi=phi: (0 if phi.shape[0] == 1 else i, 0, 0)
                )
                for phi in phis
            ]
            + [pl.BlockSpec((1, slots, EDGE, EDGE), lambda i, *_: (i, 0, 0, 0))] * 2,
            out_specs=pl.BlockSpec(
                (4 * ROWS, room * EDGE), lambda i, *_: (0, 0), pipeline_mode=pl.Buffered(1)
            ),
            scratch_shapes=[pltpu.VMEM((2 * at.blocks_per + 1, modes, 2 * EDGE), jnp.float32)],
        ),
        compiler_params=pltpu.CompilerParams(vmem_limit_bytes=56 * MIB),
        cost_estimate=cost,
    )(meta, live, row, col, *phis, k_blocks, m_blocks)


def sum_blocks(at, meta, bounds, coupling, shard, groups, right, total):
    low, high = bounds
    modes = shard.shape[1]

    def on_side(side):
        begin = jnp.maximum(meta[at.start + side], low)
        end = jnp.minimum(meta[at.start + side + 1], high)

        def bite(n):
            want = begin + n * BITE
            first = jnp.minimum(want, high - BITE)
            lane = lax.broadcasted_iota(jnp.int32, (modes, BITE * EDGE), 1) + first * EDGE
            inside = (lane >= want * EDGE) & (lane < end * EDGE)
            for g, group in enumerate(groups):
                part = shard[group[0], :, lanes(first, BITE)]
                for other in group[1:]:
                    part = part + shard[other, :, lanes(first, BITE)]
                part = jnp.where(inside, part, jnp.zeros_like(part))
                right[g * EDGE : g * EDGE + modes, :] = part
            total[side] += lax.dot_general(
                coupling[:, lanes(first, BITE)],
                right[...],
                (((1,), (1,)), ((), ())),
                preferred_element_type=jnp.float32,
            )

        up_to(jnp.maximum(end - begin + BITE - 1, 0) // BITE, bite)

    up_to(at.count + 1, on_side)


def put_products(at, groups, modes, total, out):
    for side in range(at.count + 1):
        for g in range(len(groups)):
            for flavour, (sub, part) in enumerate(
                ((side - 1, 1), (side - 1, 3), (side, 0), (side, 2))
            ):
                if 0 <= sub < at.count:
                    top, to = flavour * ROWS, (g * 4 + part) * modes
                    one = total[side, top : top + modes, g * EDGE : g * EDGE + modes]
                    out[sub, :, to : to + modes] = one.astype(out.dtype)


def grouped(sets):
    groups, taken = [], 0
    for size in sets:
        groups.append(range(taken, taken + size))
        taken += size
    return groups


def project_kernel(at, room, sets, meta, coupling, *refs):
    many = sum(sets)
    shards, refs = refs[:many], refs[many:]
    out, held, shard, right, total, held_done, shard_done = refs
    parts = [(0, room // 2), (room // 2, room)]
    coming = [[], []]
    for k, one in enumerate(shards):
        coming[0].append(pltpu.make_async_copy(one, shard.at[k], shard_done.at[k]))
    for n, (low, high) in enumerate(parts):
        to = pl.ds(low * EDGE, (high - low) * EDGE)
        coming[n].append(
            pltpu.make_async_copy(coupling.at[:, to], held.at[:, to], held_done.at[n])
        )
    for copy in coming[0] + coming[1]:
        copy.start()
    right[...] = jnp.zeros(right.shape, right.dtype)
    total[...] = jnp.zeros(total.shape, total.dtype)
    for bounds, here in zip(parts, coming):
        for copy in here:
            copy.wait()
        sum_blocks(at, meta, bounds, held, shard, grouped(sets), right, total)
    put_products(at, grouped(sets), shard.shape[1], total, out)


def project(at, meta, coupling, groups):
    flat = [shard for group in groups for shard in group]
    modes = flat[0].shape[0]
    sets = tuple(len(group) for group in groups)
    n, room = len(groups), coupling.shape[1] // EDGE
    wide = -(-n * 4 * modes // EDGE) * EDGE
    return pl.pallas_call(
        functools.partial(project_kernel, at, room, sets),
        out_shape=jax.ShapeDtypeStruct((at.count, modes, wide), coupling.dtype),
        in_specs=[pl.BlockSpec(memory_space=pltpu.SMEM)]
        + [pl.BlockSpec(memory_space=pltpu.HBM)] * (1 + len(flat)),
        out_specs=pl.BlockSpec(memory_space=pltpu.VMEM),
        scratch_shapes=[
            pltpu.VMEM(coupling.shape, coupling.dtype),
            pltpu.VMEM((len(flat), modes, coupling.shape[1]), coupling.dtype),
            pltpu.VMEM((n * EDGE, BITE * EDGE), coupling.dtype),
            pltpu.VMEM((at.count + 1, 4 * ROWS, n * EDGE), jnp.float32),
            pltpu.SemaphoreType.DMA((2,)),
            pltpu.SemaphoreType.DMA((len(flat),)),
        ],
        compiler_params=pltpu.CompilerParams(vmem_limit_bytes=56 * MIB),
        cost_estimate=LIGHT,
    )(meta, coupling, *flat)


def couple_end(at, meta, ints, places, phi_in, blocks):
    live, _, col = ints
    phis = [one[None] for one in phi_in]
    return couple(at, ROOM, meta, live, places, col, phis, *blocks, cost=HEAVY)


def assemble_kernel(modes, place, near, late, grid_k, grid_m, wide):
    own, left, right = ((near, g * 4 * modes) for g in range(3))
    second, third = ((late, g * (late.shape[2] // 2)) for g in range(2))
    plans = (
        (own, right, second, third),
        (left, own, right, second),
        (second, left, own, right),
        (third, second, left, own),
    )
    for which, grid in enumerate((grid_k, grid_m)):
        for z, plan in enumerate(plans):

            @pl.when(place[0] == z)
            def _(plan=plan, which=which):
                for far in range(2):
                    for h, (part, base) in enumerate(plan):
                        take = base + (2 * which + far) * modes
                        at = (4 * far + h) * modes
                        wide[:, :, at : at + modes] = part[:, :, take : take + modes].astype(
                            jnp.float32
                        )

        grid[...] = jnp.transpose(wide[...], (1, 0, 2))


def assemble(place, parts, modes):
    owners, rows, _ = parts[0].shape
    out = jax.ShapeDtypeStruct((rows, owners, 8 * modes), jnp.float32)
    group, tall = min(owners, 8), min(rows, TALL)
    block = pl.BlockSpec((tall, group, 8 * modes), lambda d, r, place: (r, d, 0))
    return pl.pallas_call(
        functools.partial(assemble_kernel, modes),
        out_shape=[out, out],
        grid_spec=pltpu.PrefetchScalarGridSpec(
            num_scalar_prefetch=1,
            grid=(owners // group, pl.cdiv(rows, tall)),
            in_specs=[
                pl.BlockSpec((group, tall, part.shape[2]), lambda d, r, place: (d, r, 0))
                for part in parts
            ],
            out_specs=[block] * 2,
            scratch_shapes=[pltpu.VMEM((group, tall, 8 * modes), jnp.float32)],
        ),
        compiler_params=pltpu.CompilerParams(vmem_limit_bytes=56 * MIB),
        cost_estimate=LIGHT,
    )(place, *parts)


def moved(shard, axis, by, sources=None):
    length = lax.axis_size(axis)
    sources = range(length) if sources is None else sources
    pairs = [(i, i + by) for i in sources if 0 <= i + by < length]
    return lax.ppermute(shard, axis, pairs)


def to_owners(part):
    count, modes, cols = part.shape
    owners = lax.axis_size("sub")
    part = part.reshape(owners, count * modes // owners, cols)
    return lax.all_to_all(part, "sub", split_axis=0, concat_axis=0, tiled=True)


def sent_in(phi_packed):
    last = lax.axis_size("grp") - 1
    return moved(phi_packed, "grp", 1, [0]), moved(phi_packed, "grp", -1, [last])


def sent_back(part):
    last = lax.axis_size("grp") - 1
    return lax.ppermute(part, "grp", [(1, 0), (last - 1, last)])


def both_ways(left, right):
    return moved(left, "grp", 1), moved(right, "grp", -1)


def main_path(at, lists, ints, phi, psi, border, blocks):
    meta, phi_meta, places, beside = lists
    modes = phi.shape[1]
    hold = lax.optimization_barrier

    own = pack(at, 0, ROOM, meta, psi, border)
    one = both_ways(own, own)
    own, phi, phi_meta = hold((own, phi, phi_meta))
    coupling = couple(at, ROOM, meta, *ints, [phi], *blocks)
    phi_in = sent_in(pack(at, 0, PHI_ROOM, phi_meta, phi))
    one, coupling, beside = hold((one, coupling, beside))
    last = lax.axis_size("grp") - 1
    two = (
        moved(one[0], "grp", 1, range(1, last)),
        moved(one[1], "grp", -1, range(last - 1, 0, -1)),
    )
    near = project(at, meta, coupling, [(own,), (one[0],), (one[1],)])
    near = to_owners(near)
    end = couple_end(at, meta, ints, places, phi_in, blocks)
    two, near, end = hold((two, near, end))
    third = project(at, meta, end, [two])
    third, far = hold((third, two))
    third = sent_back(third)
    second = project(at, meta, coupling, [far])
    third, second, near = hold((third, second, near))
    late = to_owners(jnp.concatenate([second, third], axis=2))
    place = lax.axis_index("grp").astype(jnp.int32)[None]
    return assemble(place, (near, late), modes), far, beside


def without(at, meta, by, room):
    kept = jnp.concatenate([meta[: at.start], jnp.full((at.start,), at.blocks_per, jnp.int32)])
    order = lax.dynamic_slice_in_dim(kept, by, at.start, 0)
    return jnp.concatenate([order, jnp.clip(meta[at.start :] - by, 0, room)])


def columns(part, modes, groups):
    part = part[:, :, : groups * 4 * modes].astype(jnp.float32)
    part = part.reshape(*part.shape[:2], groups, 2, 2, modes).transpose(3, 1, 0, 4, 2, 5)
    return part.reshape(2, *part.shape[1:3], 2 * groups * modes)


def add_kernel(old, new, out):
    out[...] = old[...] + new[...]


def added(old, new):
    rows, owners, cols = old.shape
    block = pl.BlockSpec((rows, min(owners, 8), cols), lambda d: (0, d, 0))
    return pl.pallas_call(
        add_kernel,
        out_shape=jax.ShapeDtypeStruct(old.shape, old.dtype),
        grid=(owners // min(owners, 8),),
        in_specs=[block, block],
        out_specs=block,
        input_output_aliases={0: 0},
        compiler_params=pltpu.CompilerParams(vmem_limit_bytes=32 * MIB),
    )(old, new)


def per_device(phi, psi, k_blocks, m_blocks, block_row, block_col, live):
    count, modes, width = phi.shape
    at = Meta(count, k_blocks.shape[1], width // EDGE)
    blocks = (k_blocks, m_blocks)
    ints = (live, block_row, block_col)
    border = moved(psi[count - 1], "sub", 1)
    (whole,) = listed(at, 0, block_col, live)
    phi_whole, places = listed(at, 1, block_row, live, with_places=True)
    total = at.start + count + 1
    most = lax.pmax(jnp.stack([whole[total], phi_whole[total]]), "sub")
    meta = jnp.concatenate([whole[: at.start], jnp.minimum(whole[at.start :], ROOM)])
    lists = (meta, phi_whole, places, most)
    grids, far, most = main_path(at, lists, ints, phi, psi, border, blocks)

    def turned(whole):
        return whole.transpose(1, 0, 2)

    def more(state):
        n, phi, psi, far, before = state[0], state[1], state[2], state[3], state[4:]
        phi, psi, far = lax.optimization_barrier((phi, psi, far))
        phi, psi = turned(phi), turned(psi)

        rest = without(at, whole, ROOM + n * MORE, MORE)
        packed = pack(at, 0, MORE, rest, psi, border)
        packed = jnp.stack([packed] * lax.axis_size("grp"))
        packed = lax.all_to_all(packed, "grp", split_axis=0, concat_axis=0, tiled=True)
        coupling = couple(at, MORE, rest, *ints, [phi], *blocks)
        shards = [(packed[h],) for h in range(packed.shape[0])]
        part = to_owners(project(at, rest, coupling, shards))
        after = columns(part, modes, len(shards))

        skipped = (n + 1) * PHI_ROOM
        rest = without(at, phi_whole, skipped, PHI_ROOM)
        phi_in = sent_in(pack(at, 0, PHI_ROOM, rest, phi))
        end = couple_end(at, meta, ints, places - skipped, phi_in, blocks)
        part = project(at, meta, end, [far])
        part = columns(to_owners(sent_back(part)), modes, 1)
        place, zero = lax.axis_index("grp"), jnp.zeros_like(part[..., :modes])
        last = lax.axis_size("grp") - 1
        ends = []
        for low in (0, modes):
            one = part[..., low : low + modes]
            for h in range(last + 1):
                wanted = ((place == 0) & (h == last)) | ((place == last) & (h == 0))
                ends.append(jnp.where(wanted, one, zero))
        after = after + jnp.concatenate(ends, axis=-1)
        return (n + 1, *state[1:4], *(added(old, new) for old, new in zip(before, after)))

    def unfinished(state):
        psi_left = ROOM + state[0] * MORE < most[0]
        return psi_left | ((state[0] + 1) * PHI_ROOM < most[1])

    state = (jnp.int32(0), turned(phi), turned(psi), far, *grids)
    state = lax.while_loop(unfinished, more, state)
    return tuple(turned(grid)[None, None] for grid in state[4:])


def solution(mesh):
    placed = (
        P("sub", "grp", None),
        P("sub", "grp", None),
        P("sub", None, None, None),
        P("sub", None, None, None),
        P("sub", None),
        P("sub", None),
        P("sub"),
    )
    return jax.shard_map(
        per_device,
        mesh=mesh,
        in_specs=placed,
        out_specs=(P("sub", "grp", None, None, None), P("sub", "grp", None, None, None)),
        check_vma=False,
    )
```

```python
import functools

import jax
import jax.numpy as jnp
from jax import lax
from jax.experimental import pallas as pl
from jax.experimental.pallas import tpu as pltpu
from jax.sharding import PartitionSpec as P

EDGE = 128
ROWS = 112
SLOTS = 4
BITE = 4
ROOM = 94
PHI_ROOM = 92
MORE = 16
TALL = 32
MIB = 1 << 20
LIGHT = pl.CostEstimate(flops=1, bytes_accessed=1, transcendentals=0)
HEAVY = pl.CostEstimate(flops=25_000_000_000, bytes_accessed=1, transcendentals=0)


def up_to(limit, body, unroll=1):
    lax.fori_loop(0, limit, lambda n, _: (body(n), 0)[1], 0, unroll=unroll)


def lanes(block, count=1):
    return pl.ds(pl.multiple_of(block * EDGE, EDGE), count * EDGE)


class Meta:
    def __init__(self, count, slots, blocks_per):
        self.count, self.slots, self.blocks_per = count, slots, blocks_per
        self.keys = (count + 1) * blocks_per
        self.order = 0
        self.start = self.keys + max(ROOM + MORE, 2 * PHI_ROOM)
        self.size = self.start + count + 2


def list_kernel(at, shift, live, block, meta, *refs):
    (*places, flags) = refs

    def clear(n):
        flags[n] = 0

    up_to(at.keys, clear, unroll=16)
    for i in range(at.count):

        def mark(n, i=i):
            flags[block[i, n] + (i + shift) * at.blocks_per] = 1

        up_to(live[i], mark)

    def place(key, taken):
        needed = flags[key]
        meta[at.order + taken] = key
        flags[key] = taken
        return taken + needed

    taken = 0
    for side in range(at.count + 1):
        meta[at.start + side] = taken
        taken = lax.fori_loop(
            side * at.blocks_per, (side + 1) * at.blocks_per, place, taken, unroll=at.blocks_per
        )
    meta[at.start + at.count + 1] = taken

    for found in places:
        for i in range(at.count):

            def find(n, i=i, found=found):
                found[i, n] = flags[block[i, n] + (i + shift) * at.blocks_per]

            up_to(live[i], find)


def listed(at, shift, block, live, with_places=False):
    out = [jax.ShapeDtypeStruct((at.size,), jnp.int32)]
    if with_places:
        out.append(jax.ShapeDtypeStruct(block.shape, jnp.int32))
    return pl.pallas_call(
        functools.partial(list_kernel, at, shift),
        out_shape=out,
        in_specs=[pl.BlockSpec(memory_space=pltpu.SMEM)] * 2,
        out_specs=[pl.BlockSpec(memory_space=pltpu.SMEM)] * len(out),
        scratch_shapes=[pltpu.SMEM((at.keys,), jnp.int32)],
        cost_estimate=LIGHT,
    )(live, block)


def pack_kernel(at, first, room, meta, *refs):
    borders, psi, out = refs[:-2], refs[-2], refs[-1]
    split = jnp.clip(meta[at.start + 1] - first, 0, room)
    end = jnp.clip(meta[at.start + at.count + 1] - first, 0, room)

    def from_border(c):
        for border in borders:
            out[:, lanes(c)] = border[:, lanes(meta[at.order + first + c])]

    def from_psi(c):
        key = meta[at.order + first + c]
        out[:, lanes(c)] = psi[key // at.blocks_per - 1, :, lanes(key % at.blocks_per)]

    def from_none(c):
        out[:, lanes(c)] = jnp.zeros((out.shape[0], EDGE), out.dtype)

    up_to(split, from_border)
    up_to(end - split, lambda c: from_psi(split + c))
    up_to(room - end, lambda c: from_none(end + c))


def pack(at, first, room, meta, psi, *borders):
    return pl.pallas_call(
        functools.partial(pack_kernel, at, first, room),
        out_shape=jax.ShapeDtypeStruct((psi.shape[1], room * EDGE), psi.dtype),
        in_specs=[pl.BlockSpec(memory_space=pltpu.SMEM)]
        + [pl.BlockSpec(memory_space=pltpu.VMEM)] * (1 + len(borders)),
        out_specs=pl.BlockSpec(memory_space=pltpu.VMEM),
        compiler_params=pltpu.CompilerParams(vmem_limit_bytes=8 * MIB),
        cost_estimate=LIGHT,
    )(meta, *borders, psi)


def coupling_kernel(at, room, many, meta, live, row, col, *refs):
    phis, (k_blocks, m_blocks, out, total) = refs[:many], refs[many:]
    i = pl.program_id(0)
    couple_one(at, room, i, meta, live, row, col, phis, k_blocks, m_blocks, out, total)


def couple_one(at, room, i, meta, live, row, col, phis, k_blocks, m_blocks, out, total):
    modes, blocks = phis[0].shape[1], phis[0].shape[2] // EDGE
    here, middle, end = (meta[at.start + i + n] for n in range(3))
    first = at.blocks_per * i

    def clear(n):
        total[meta[at.order + here + n] - first] = jnp.zeros(total.shape[1:], total.dtype)

    up_to(end - here, clear)

    def add_slots(step):
        terms = []
        for n in range(SLOTS):
            slot = jnp.minimum(step * SLOTS + n, at.slots - 1)
            where = row[i, slot]
            here = (step * SLOTS + n < live[i]) & (where >= 0) & (where < blocks)
            which = lanes(jnp.clip(where, 0, blocks - 1))
            picked = sum([phi[0, :, which] for phi in phis[1:]], phis[0][0, :, which])
            both = jnp.concatenate([k_blocks[0, slot], m_blocks[0, slot]], axis=1)
            to = jnp.where(here, col[i, slot], 2 * at.blocks_per)
            terms.append((to, jnp.dot(picked, both, preferred_element_type=jnp.float32)))
        for to, term in terms:
            total[to] += term

    up_to((live[i] + SLOTS - 1) // SLOTS, add_slots)

    def put(flavour, c):
        done = total[meta[at.order + c] - first].astype(out.dtype)
        out[flavour * ROWS : flavour * ROWS + modes, lanes(c)] = done[:, :EDGE]
        out[(flavour + 1) * ROWS : (flavour + 1) * ROWS + modes, lanes(c)] = done[:, EDGE:]

    def blank(top, c):
        out[top : top + 2 * ROWS, lanes(c)] = jnp.zeros((2 * ROWS, EDGE), out.dtype)

    up_to(middle - here, lambda n: put(2, here + n))
    up_to(end - middle, lambda n: put(0, middle + n))

    @pl.when(i == 0)
    def _():
        up_to(middle, lambda n: blank(0, n))

    @pl.when(i == at.count - 1)
    def _():
        up_to(room - middle, lambda n: blank(2 * ROWS, middle + n))
        up_to(room - end, lambda n: blank(0, end + n))


def couple(at, room, meta, live, row, col, phis, k_blocks, m_blocks, cost=LIGHT):
    _, modes, width = phis[0].shape
    count, slots = k_blocks.shape[:2]
    return pl.pallas_call(
        functools.partial(coupling_kernel, at, room, len(phis)),
        out_shape=jax.ShapeDtypeStruct((4 * ROWS, room * EDGE), phis[0].dtype),
        grid_spec=pltpu.PrefetchScalarGridSpec(
            num_scalar_prefetch=4,
            grid=(count,),
            in_specs=[
                pl.BlockSpec(
                    (1, modes, width), lambda i, *_, phi=phi: (0 if phi.shape[0] == 1 else i, 0, 0)
                )
                for phi in phis
            ]
            + [pl.BlockSpec((1, slots, EDGE, EDGE), lambda i, *_: (i, 0, 0, 0))] * 2,
            out_specs=pl.BlockSpec(
                (4 * ROWS, room * EDGE), lambda i, *_: (0, 0), pipeline_mode=pl.Buffered(1)
            ),
            scratch_shapes=[pltpu.VMEM((2 * at.blocks_per + 1, modes, 2 * EDGE), jnp.float32)],
        ),
        compiler_params=pltpu.CompilerParams(vmem_limit_bytes=56 * MIB),
        cost_estimate=cost,
    )(meta, live, row, col, *phis, k_blocks, m_blocks)


def sum_blocks(at, meta, bounds, couplings, shard, groups, right, totals):
    low, high = bounds
    modes = shard.shape[1]

    def on_side(side):
        begin = jnp.maximum(meta[at.start + side], low)
        end = jnp.minimum(meta[at.start + side + 1], high)

        def bite(n):
            want = begin + n * BITE
            first = jnp.minimum(want, high - BITE)
            lane = lax.broadcasted_iota(jnp.int32, (modes, BITE * EDGE), 1) + first * EDGE
            inside = (lane >= want * EDGE) & (lane < end * EDGE)
            for g, group in enumerate(groups):
                part = shard[group[0], :, lanes(first, BITE)]
                for other in group[1:]:
                    part = part + shard[other, :, lanes(first, BITE)]
                part = jnp.where(inside, part, jnp.zeros_like(part))
                right[g * EDGE : g * EDGE + modes, :] = part
            for coupling, total in zip(couplings, totals):
                total[side] += lax.dot_general(
                    coupling[:, lanes(first, BITE)],
                    right[...],
                    (((1,), (1,)), ((), ())),
                    preferred_element_type=jnp.float32,
                )

        up_to(jnp.maximum(end - begin + BITE - 1, 0) // BITE, bite)

    up_to(at.count + 1, on_side)


def put_products(at, groups, modes, total, out):
    for side in range(at.count + 1):
        for g in range(len(groups)):
            for flavour, (sub, part) in enumerate(
                ((side - 1, 1), (side - 1, 3), (side, 0), (side, 2))
            ):
                if 0 <= sub < at.count:
                    top, to = flavour * ROWS, (g * 4 + part) * modes
                    one = total[side, top : top + modes, g * EDGE : g * EDGE + modes]
                    out[sub, :, to : to + modes] = one.astype(out.dtype)


def grouped(sets):
    groups, taken = [], 0
    for size in sets:
        groups.append(range(taken, taken + size))
        taken += size
    return groups


def project_kernel(at, room, sets, many, meta, *refs):
    couplings, refs = refs[:many], refs[many:]
    shards, refs = refs[: sum(sets)], refs[sum(sets) :]
    outs, refs = refs[:many], refs[many:]
    helds, totals, (shard, right, held_done, shard_done) = refs[:many], refs[many : 2 * many], refs[2 * many :]
    parts = [(0, room // 2), (room // 2, room)]
    coming = [[], []]
    for k, one in enumerate(shards):
        coming[0].append(pltpu.make_async_copy(one, shard.at[k], shard_done.at[k]))
    for n, (low, high) in enumerate(parts):
        to = pl.ds(low * EDGE, (high - low) * EDGE)
        for k, (coupling, held) in enumerate(zip(couplings, helds)):
            coming[n].append(
                pltpu.make_async_copy(coupling.at[:, to], held.at[:, to], held_done.at[2 * k + n])
            )
    for copy in coming[0] + coming[1]:
        copy.start()
    right[...] = jnp.zeros(right.shape, right.dtype)
    for total in totals:
        total[...] = jnp.zeros(total.shape, total.dtype)
    for bounds, here in zip(parts, coming):
        for copy in here:
            copy.wait()
        sum_blocks(at, meta, bounds, helds, shard, grouped(sets), right, totals)
    for total, out in zip(totals, outs):
        put_products(at, grouped(sets), shard.shape[1], total, out)


def project(at, meta, couplings, groups):
    flat = [shard for group in groups for shard in group]
    modes, held = flat[0].shape[0], couplings[0]
    sets = tuple(len(group) for group in groups)
    n, many, room = len(groups), len(couplings), held.shape[1] // EDGE
    wide = -(-n * 4 * modes // EDGE) * EDGE
    return pl.pallas_call(
        functools.partial(project_kernel, at, room, sets, many),
        out_shape=[jax.ShapeDtypeStruct((at.count, modes, wide), held.dtype)] * many,
        in_specs=[pl.BlockSpec(memory_space=pltpu.SMEM)]
        + [pl.BlockSpec(memory_space=pltpu.HBM)] * (many + len(flat)),
        out_specs=[pl.BlockSpec(memory_space=pltpu.VMEM)] * many,
        scratch_shapes=[pltpu.VMEM(held.shape, held.dtype)] * many
        + [pltpu.VMEM((at.count + 1, 4 * ROWS, n * EDGE), jnp.float32)] * many
        + [
            pltpu.VMEM((len(flat), modes, held.shape[1]), held.dtype),
            pltpu.VMEM((n * EDGE, BITE * EDGE), held.dtype),
            pltpu.SemaphoreType.DMA((2 * many,)),
            pltpu.SemaphoreType.DMA((len(flat),)),
        ],
        compiler_params=pltpu.CompilerParams(vmem_limit_bytes=56 * MIB),
        cost_estimate=LIGHT,
    )(meta, *couplings, *flat)


def couple_end(at, meta, ints, places, phi_in, blocks):
    live, _, col = ints
    phis = [one[None] for one in phi_in]
    return couple(at, ROOM, meta, live, places, col, phis, *blocks, cost=HEAVY)


def assemble_kernel(modes, place, near, second, third, grid_k, grid_m, wide):
    own, left, right = ((near, g * 4 * modes) for g in range(3))
    second, third = (second, 0), (third, 0)
    plans = (
        (own, right, second, third),
        (left, own, right, second),
        (second, left, own, right),
        (third, second, left, own),
    )
    for which, grid in enumerate((grid_k, grid_m)):
        for z, plan in enumerate(plans):

            @pl.when(place[0] == z)
            def _(plan=plan, which=which):
                for far in range(2):
                    for h, (part, base) in enumerate(plan):
                        take = base + (2 * which + far) * modes
                        at = (4 * far + h) * modes
                        wide[:, :, at : at + modes] = part[:, :, take : take + modes].astype(
                            jnp.float32
                        )

        grid[...] = jnp.transpose(wide[...], (1, 0, 2))


def assemble(place, parts, modes):
    owners, rows, _ = parts[0].shape
    out = jax.ShapeDtypeStruct((rows, owners, 8 * modes), jnp.float32)
    group, tall = min(owners, 8), min(rows, TALL)
    block = pl.BlockSpec((tall, group, 8 * modes), lambda d, r, place: (r, d, 0))
    return pl.pallas_call(
        functools.partial(assemble_kernel, modes),
        out_shape=[out, out],
        grid_spec=pltpu.PrefetchScalarGridSpec(
            num_scalar_prefetch=1,
            grid=(owners // group, pl.cdiv(rows, tall)),
            in_specs=[
                pl.BlockSpec((group, tall, part.shape[2]), lambda d, r, place: (d, r, 0))
                for part in parts
            ],
            out_specs=[block] * 2,
            scratch_shapes=[pltpu.VMEM((group, tall, 8 * modes), jnp.float32)],
        ),
        compiler_params=pltpu.CompilerParams(vmem_limit_bytes=56 * MIB),
        cost_estimate=LIGHT,
    )(place, *parts)


def moved(shard, axis, by, sources=None):
    length = lax.axis_size(axis)
    sources = range(length) if sources is None else sources
    pairs = [(i, i + by) for i in sources if 0 <= i + by < length]
    return lax.ppermute(shard, axis, pairs)


def to_owners(part):
    count, modes, cols = part.shape
    owners = lax.axis_size("sub")
    part = part.reshape(owners, count * modes // owners, cols)
    return lax.all_to_all(part, "sub", split_axis=0, concat_axis=0, tiled=True)


def sent_in(phi_packed):
    last = lax.axis_size("grp") - 1
    return moved(phi_packed, "grp", 1, [0]), moved(phi_packed, "grp", -1, [last])


def sent_back(part):
    last = lax.axis_size("grp") - 1
    return lax.ppermute(part, "grp", [(1, 0), (last - 1, last)])


def both_ways(left, right):
    return moved(left, "grp", 1), moved(right, "grp", -1)


def main_path(at, lists, ints, phi, psi, border, blocks):
    meta, phi_meta, places, beside = lists
    modes = phi.shape[1]
    hold = lax.optimization_barrier

    own = pack(at, 0, ROOM, meta, psi, border)
    one = both_ways(own, own)
    own, phi, phi_meta = hold((own, phi, phi_meta))
    coupling = couple(at, ROOM, meta, *ints, [phi], *blocks)
    phi_in = sent_in(pack(at, 0, PHI_ROOM, phi_meta, phi))
    one, coupling, beside = hold((one, coupling, beside))
    last = lax.axis_size("grp") - 1
    two = (
        moved(one[0], "grp", 1, range(1, last)),
        moved(one[1], "grp", -1, range(last - 1, 0, -1)),
    )
    (near,) = project(at, meta, [coupling], [(own,), (one[0],), (one[1],)])
    near = to_owners(near)
    end = couple_end(at, meta, ints, places, phi_in, blocks)
    two, near, end = hold((two, near, end))
    second, third = project(at, meta, [coupling, end], [two])
    third = sent_back(third)
    second = to_owners(second)
    third, second, near = hold((third, second, near))
    third = to_owners(third)
    place = lax.axis_index("grp").astype(jnp.int32)[None]
    return assemble(place, (near, second, third), modes), two, beside


def without(at, meta, by, room):
    kept = jnp.concatenate([meta[: at.start], jnp.full((at.start,), at.blocks_per, jnp.int32)])
    order = lax.dynamic_slice_in_dim(kept, by, at.start, 0)
    return jnp.concatenate([order, jnp.clip(meta[at.start :] - by, 0, room)])


def columns(part, modes, groups):
    part = part[:, :, : groups * 4 * modes].astype(jnp.float32)
    part = part.reshape(*part.shape[:2], groups, 2, 2, modes).transpose(3, 1, 0, 4, 2, 5)
    return part.reshape(2, *part.shape[1:3], 2 * groups * modes)


def add_kernel(old, new, out):
    out[...] = old[...] + new[...]


def added(old, new):
    rows, owners, cols = old.shape
    block = pl.BlockSpec((rows, min(owners, 8), cols), lambda d: (0, d, 0))
    return pl.pallas_call(
        add_kernel,
        out_shape=jax.ShapeDtypeStruct(old.shape, old.dtype),
        grid=(owners // min(owners, 8),),
        in_specs=[block, block],
        out_specs=block,
        input_output_aliases={0: 0},
        compiler_params=pltpu.CompilerParams(vmem_limit_bytes=32 * MIB),
    )(old, new)


def per_device(phi, psi, k_blocks, m_blocks, block_row, block_col, live):
    count, modes, width = phi.shape
    at = Meta(count, k_blocks.shape[1], width // EDGE)
    blocks = (k_blocks, m_blocks)
    ints = (live, block_row, block_col)
    border = moved(psi[count - 1], "sub", 1)
    (whole,) = listed(at, 0, block_col, live)
    phi_whole, places = listed(at, 1, block_row, live, with_places=True)
    total = at.start + count + 1
    most = lax.pmax(jnp.stack([whole[total], phi_whole[total]]), "sub")
    over = jnp.maximum(most - jnp.asarray([ROOM, PHI_ROOM], jnp.int32), 0)
    each = jnp.asarray([MORE, PHI_ROOM], jnp.int32)
    trips = jnp.max((over + each - 1) // each)
    meta = jnp.concatenate([whole[: at.start], jnp.minimum(whole[at.start :], ROOM)])
    lists = (meta, phi_whole, places, trips)
    grids, far, trips = main_path(at, lists, ints, phi, psi, border, blocks)

    def turned(whole):
        return whole.transpose(1, 0, 2)

    def more(state):
        n, phi, psi, far, before = state[0], state[1], state[2], state[3], state[4:]
        phi, psi, far = lax.optimization_barrier((phi, psi, far))
        phi, psi = turned(phi), turned(psi)

        rest = without(at, whole, ROOM + n * MORE, MORE)
        packed = pack(at, 0, MORE, rest, psi, border)
        packed = jnp.stack([packed] * lax.axis_size("grp"))
        packed = lax.all_to_all(packed, "grp", split_axis=0, concat_axis=0, tiled=True)
        coupling = couple(at, MORE, rest, *ints, [phi], *blocks)
        shards = [(packed[h],) for h in range(packed.shape[0])]
        part = to_owners(project(at, rest, [coupling], shards)[0])
        after = columns(part, modes, len(shards))

        skipped = (n + 1) * PHI_ROOM
        rest = without(at, phi_whole, skipped, PHI_ROOM)
        phi_in = sent_in(pack(at, 0, PHI_ROOM, rest, phi))
        end = couple_end(at, meta, ints, places - skipped, phi_in, blocks)
        (part,) = project(at, meta, [end], [far])
        part = columns(to_owners(sent_back(part)), modes, 1)
        place, zero = lax.axis_index("grp"), jnp.zeros_like(part[..., :modes])
        last = lax.axis_size("grp") - 1
        ends = []
        for low in (0, modes):
            one = part[..., low : low + modes]
            for h in range(last + 1):
                wanted = ((place == 0) & (h == last)) | ((place == last) & (h == 0))
                ends.append(jnp.where(wanted, one, zero))
        after = after + jnp.concatenate(ends, axis=-1)
        return (n + 1, *state[1:4], *(added(old, new) for old, new in zip(before, after)))

    state = (jnp.int32(0), turned(phi), turned(psi), far, *grids)
    state = lax.while_loop(lambda state: state[0] < trips, more, state)
    return tuple(turned(grid)[None, None] for grid in state[4:])


def solution(mesh):
    placed = (
        P("sub", "grp", None),
        P("sub", "grp", None),
        P("sub", None, None, None),
        P("sub", None, None, None),
        P("sub", None),
        P("sub", None),
        P("sub"),
    )
    return jax.shard_map(
        per_device,
        mesh=mesh,
        in_specs=placed,
        out_specs=(P("sub", "grp", None, None, None), P("sub", "grp", None, None, None)),
        check_vma=False,
    )
```

```python
import functools

import jax
import jax.numpy as jnp
from jax import lax
from jax.experimental import pallas as pl
from jax.experimental.pallas import tpu as pltpu
from jax.sharding import PartitionSpec as P

EDGE = 128
ROWS = 112
SLOTS = 8
BITE = 4
ROOM = 94
PHI_ROOM = 92
MORE = 16
TALL = 32
MIB = 1 << 20
LIGHT = pl.CostEstimate(flops=1, bytes_accessed=1, transcendentals=0)
HEAVY = pl.CostEstimate(flops=25_000_000_000, bytes_accessed=1, transcendentals=0)


def up_to(limit, body, unroll=1):
    lax.fori_loop(0, limit, lambda n, _: (body(n), 0)[1], 0, unroll=unroll)


def by_four(limit, body):
    def four(step):
        for k in range(4):
            body(jnp.minimum(step * 4 + k, limit - 1))

    up_to((limit + 3) // 4, four)


def lanes(block, count=1):
    return pl.ds(pl.multiple_of(block * EDGE, EDGE), count * EDGE)


class Meta:
    def __init__(self, count, slots, blocks_per):
        self.count, self.slots, self.blocks_per = count, slots, blocks_per
        self.keys = (count + 1) * blocks_per
        self.order = 0
        self.start = self.keys + max(ROOM + MORE, 2 * PHI_ROOM)
        self.size = self.start + count + 2


def list_kernel(at, shift, live, block, meta, *refs):
    (*places, flags) = refs

    def clear(n):
        flags[n] = 0

    up_to(at.keys, clear, unroll=16)
    for i in range(at.count):

        def mark(n, i=i):
            flags[block[i, n] + (i + shift) * at.blocks_per] = 1

        up_to(live[i], mark)

    def place(key, taken):
        needed = flags[key]
        meta[at.order + taken] = key
        flags[key] = taken
        return taken + needed

    taken = 0
    for side in range(at.count + 1):
        meta[at.start + side] = taken
        taken = lax.fori_loop(
            side * at.blocks_per, (side + 1) * at.blocks_per, place, taken, unroll=at.blocks_per
        )
    meta[at.start + at.count + 1] = taken

    for found in places:
        for i in range(at.count):

            def find(n, i=i, found=found):
                found[i, n] = flags[block[i, n] + (i + shift) * at.blocks_per]

            up_to(live[i], find)


def listed(at, shift, block, live, with_places=False):
    out = [jax.ShapeDtypeStruct((at.size,), jnp.int32)]
    if with_places:
        out.append(jax.ShapeDtypeStruct(block.shape, jnp.int32))
    return pl.pallas_call(
        functools.partial(list_kernel, at, shift),
        out_shape=out,
        in_specs=[pl.BlockSpec(memory_space=pltpu.SMEM)] * 2,
        out_specs=[pl.BlockSpec(memory_space=pltpu.SMEM)] * len(out),
        scratch_shapes=[pltpu.SMEM((at.keys,), jnp.int32)],
        cost_estimate=LIGHT,
    )(live, block)


def pack_kernel(at, first, room, meta, *refs):
    borders, psi, out = refs[:-2], refs[-2], refs[-1]
    split = jnp.clip(meta[at.start + 1] - first, 0, room)
    end = jnp.clip(meta[at.start + at.count + 1] - first, 0, room)

    def from_border(c):
        for border in borders:
            out[:, lanes(c)] = border[:, lanes(meta[at.order + first + c])]

    def from_psi(c):
        key = meta[at.order + first + c]
        out[:, lanes(c)] = psi[key // at.blocks_per - 1, :, lanes(key % at.blocks_per)]

    def from_none(c):
        out[:, lanes(c)] = jnp.zeros((out.shape[0], EDGE), out.dtype)

    up_to(split, from_border)
    up_to(end - split, lambda c: from_psi(split + c))
    up_to(room - end, lambda c: from_none(end + c))


def pack(at, first, room, meta, psi, *borders):
    return pl.pallas_call(
        functools.partial(pack_kernel, at, first, room),
        out_shape=jax.ShapeDtypeStruct((psi.shape[1], room * EDGE), psi.dtype),
        in_specs=[pl.BlockSpec(memory_space=pltpu.SMEM)]
        + [pl.BlockSpec(memory_space=pltpu.VMEM)] * (1 + len(borders)),
        out_specs=pl.BlockSpec(memory_space=pltpu.VMEM),
        compiler_params=pltpu.CompilerParams(vmem_limit_bytes=8 * MIB),
        cost_estimate=LIGHT,
    )(meta, *borders, psi)


def coupling_kernel(at, room, many, meta, live, row, col, *refs):
    phis, (k_blocks, m_blocks, out, total) = refs[:many], refs[many:]
    i = pl.program_id(0)
    couple_one(at, room, i, meta, live, row, col, phis, k_blocks, m_blocks, out, total)


def couple_one(at, room, i, meta, live, row, col, phis, k_blocks, m_blocks, out, total):
    modes, blocks = phis[0].shape[1], phis[0].shape[2] // EDGE
    here, middle, end = (meta[at.start + i + n] for n in range(3))
    first = at.blocks_per * i

    def clear(n):
        total[meta[at.order + here + n] - first] = jnp.zeros(total.shape[1:], total.dtype)

    by_four(end - here, clear)

    def add_slots(step):
        terms = []
        for n in range(SLOTS):
            slot = jnp.minimum(step * SLOTS + n, at.slots - 1)
            where = row[i, slot]
            here = (step * SLOTS + n < live[i]) & (where >= 0) & (where < blocks)
            which = lanes(jnp.clip(where, 0, blocks - 1))
            picked = sum([phi[0, :, which] for phi in phis[1:]], phis[0][0, :, which])
            both = jnp.concatenate([k_blocks[0, slot], m_blocks[0, slot]], axis=1)
            to = jnp.where(here, col[i, slot], 2 * at.blocks_per)
            terms.append((to, jnp.dot(picked, both, preferred_element_type=jnp.float32)))
        for to, term in terms:
            total[to] += term

    up_to((live[i] + SLOTS - 1) // SLOTS, add_slots)

    def put(flavour, c):
        done = total[meta[at.order + c] - first].astype(out.dtype)
        out[flavour * ROWS : flavour * ROWS + modes, lanes(c)] = done[:, :EDGE]
        out[(flavour + 1) * ROWS : (flavour + 1) * ROWS + modes, lanes(c)] = done[:, EDGE:]

    def blank(top, c):
        out[top : top + 2 * ROWS, lanes(c)] = jnp.zeros((2 * ROWS, EDGE), out.dtype)

    by_four(middle - here, lambda n: put(2, here + n))
    by_four(end - middle, lambda n: put(0, middle + n))

    @pl.when(i == 0)
    def _():
        up_to(middle, lambda n: blank(0, n))

    @pl.when(i == at.count - 1)
    def _():
        up_to(room - middle, lambda n: blank(2 * ROWS, middle + n))
        up_to(room - end, lambda n: blank(0, end + n))


def couple(at, room, meta, live, row, col, phis, k_blocks, m_blocks, cost=LIGHT):
    _, modes, width = phis[0].shape
    count, slots = k_blocks.shape[:2]
    return pl.pallas_call(
        functools.partial(coupling_kernel, at, room, len(phis)),
        out_shape=jax.ShapeDtypeStruct((4 * ROWS, room * EDGE), phis[0].dtype),
        grid_spec=pltpu.PrefetchScalarGridSpec(
            num_scalar_prefetch=4,
            grid=(count,),
            in_specs=[
                pl.BlockSpec(
                    (1, modes, width), lambda i, *_, phi=phi: (0 if phi.shape[0] == 1 else i, 0, 0)
                )
                for phi in phis
            ]
            + [pl.BlockSpec((1, slots, EDGE, EDGE), lambda i, *_: (i, 0, 0, 0))] * 2,
            out_specs=pl.BlockSpec(
                (4 * ROWS, room * EDGE), lambda i, *_: (0, 0), pipeline_mode=pl.Buffered(1)
            ),
            scratch_shapes=[pltpu.VMEM((2 * at.blocks_per + 1, modes, 2 * EDGE), jnp.float32)],
        ),
        compiler_params=pltpu.CompilerParams(vmem_limit_bytes=56 * MIB),
        cost_estimate=cost,
    )(meta, live, row, col, *phis, k_blocks, m_blocks)


def sum_blocks(at, meta, bounds, couplings, shard, groups, right, totals):
    low, high = bounds
    modes = shard.shape[1]

    def on_side(side):
        begin = jnp.maximum(meta[at.start + side], low)
        end = jnp.minimum(meta[at.start + side + 1], high)

        def bite(n):
            want = begin + n * BITE
            first = jnp.minimum(want, high - BITE)
            lane = lax.broadcasted_iota(jnp.int32, (modes, BITE * EDGE), 1) + first * EDGE
            inside = (lane >= want * EDGE) & (lane < end * EDGE)
            for g, group in enumerate(groups):
                part = shard[group[0], :, lanes(first, BITE)]
                for other in group[1:]:
                    part = part + shard[other, :, lanes(first, BITE)]
                part = jnp.where(inside, part, jnp.zeros_like(part))
                right[g * EDGE : g * EDGE + modes, :] = part
            for coupling, total in zip(couplings, totals):
                total[side] += lax.dot_general(
                    coupling[:, lanes(first, BITE)],
                    right[...],
                    (((1,), (1,)), ((), ())),
                    preferred_element_type=jnp.float32,
                )

        up_to(jnp.maximum(end - begin + BITE - 1, 0) // BITE, bite)

    up_to(at.count + 1, on_side)


def put_products(at, groups, modes, total, out):
    for side in range(at.count + 1):
        for g in range(len(groups)):
            for flavour, (sub, part) in enumerate(
                ((side - 1, 1), (side - 1, 3), (side, 0), (side, 2))
            ):
                if 0 <= sub < at.count:
                    top, to = flavour * ROWS, (g * 4 + part) * modes
                    one = total[side, top : top + modes, g * EDGE : g * EDGE + modes]
                    out[sub, :modes, to : to + modes] = one.astype(out.dtype)


def grouped(sets):
    groups, taken = [], 0
    for size in sets:
        groups.append(range(taken, taken + size))
        taken += size
    return groups


def put_spread(at, modes, me, total, outs):
    for k, out in enumerate(outs):
        sub = jnp.bitwise_xor(me, k)
        for part, (side, flavour) in enumerate(((sub, 2), (sub + 1, 0), (sub, 3), (sub + 1, 1))):
            one = total[side, flavour * ROWS : flavour * ROWS + modes, :modes]
            out[:modes, part * modes : (part + 1) * modes] = one.astype(out.dtype)


def project_kernel(at, room, sets, many, spread, meta, me, *refs):
    couplings, refs = refs[:many], refs[many:]
    shards, refs = refs[: sum(sets)], refs[sum(sets) :]
    pieces = at.count if spread else 0
    outs, spreads, refs = refs[:many], refs[many - 1 : many - 1 + pieces], refs[many + max(pieces - 1, 0) :]
    helds, totals, (shard, right, held_done, shard_done) = refs[:many], refs[many : 2 * many], refs[2 * many :]
    parts = [(0, room // 2), (room // 2, room)]
    coming = [[], []]
    for k, one in enumerate(shards):
        coming[0].append(pltpu.make_async_copy(one, shard.at[k], shard_done.at[k]))
    for n, (low, high) in enumerate(parts):
        to = pl.ds(low * EDGE, (high - low) * EDGE)
        for k, (coupling, held) in enumerate(zip(couplings, helds)):
            coming[n].append(
                pltpu.make_async_copy(coupling.at[:, to], held.at[:, to], held_done.at[2 * k + n])
            )
    for copy in coming[0] + coming[1]:
        copy.start()
    right[...] = jnp.zeros(right.shape, right.dtype)
    for total in totals:
        total[...] = jnp.zeros(total.shape, total.dtype)
    for bounds, here in zip(parts, coming):
        for copy in here:
            copy.wait()
        sum_blocks(at, meta, bounds, helds, shard, grouped(sets), right, totals)
    for n, (total, out) in enumerate(zip(totals, outs)):
        if spread and n == many - 1:
            put_spread(at, shard.shape[1], me[0], total, spreads)
        else:
            put_products(at, grouped(sets), shard.shape[1], total, out)


def project(at, meta, couplings, groups, spread=False):
    flat = [shard for group in groups for shard in group]
    modes, held = flat[0].shape[0], couplings[0]
    sets = tuple(len(group) for group in groups)
    n, many, room = len(groups), len(couplings), held.shape[1] // EDGE
    wide = -(-n * 4 * modes // EDGE) * EDGE
    tall = -(-modes // 8) * 8
    out = [jax.ShapeDtypeStruct((at.count, tall, wide), held.dtype)] * many
    if spread:
        out = out[:-1] + [jax.ShapeDtypeStruct((tall, wide), held.dtype)] * at.count
    me = lax.axis_index("sub").astype(jnp.int32)[None]
    return pl.pallas_call(
        functools.partial(project_kernel, at, room, sets, many, spread),
        out_shape=out,
        in_specs=[pl.BlockSpec(memory_space=pltpu.SMEM)] * 2
        + [pl.BlockSpec(memory_space=pltpu.HBM)] * (many + len(flat)),
        out_specs=[pl.BlockSpec(memory_space=pltpu.VMEM)] * len(out),
        scratch_shapes=[pltpu.VMEM(held.shape, held.dtype)] * many
        + [pltpu.VMEM((at.count + 1, 4 * ROWS, n * EDGE), jnp.float32)] * many
        + [
            pltpu.VMEM((len(flat), modes, held.shape[1]), held.dtype),
            pltpu.VMEM((n * EDGE, BITE * EDGE), held.dtype),
            pltpu.SemaphoreType.DMA((2 * many,)),
            pltpu.SemaphoreType.DMA((len(flat),)),
        ],
        compiler_params=pltpu.CompilerParams(vmem_limit_bytes=56 * MIB),
        cost_estimate=LIGHT,
    )(meta, me, *couplings, *flat)


def couple_end(at, meta, ints, places, phi_in, blocks):
    live, _, col = ints
    phis = [one[None] for one in phi_in]
    return couple(at, ROOM, meta, live, places, col, phis, *blocks, cost=HEAVY)


def assemble_kernel(modes, place, near, second, *refs):
    thirds, (grid_k, grid_m, wide, sorted_third) = refs[:-4], refs[-4:]
    third = thirds[0]
    if len(thirds) > 1:
        third = sorted_third
        for k, one in enumerate(thirds):
            third[jnp.bitwise_xor(place[1], k)] = one[...]
    own, left, right = ((near, g * 4 * modes) for g in range(3))
    second, third = (second, 0), (third, 0)
    plans = (
        (own, right, second, third),
        (left, own, right, second),
        (second, left, own, right),
        (third, second, left, own),
    )
    for which, grid in enumerate((grid_k, grid_m)):
        for z, plan in enumerate(plans):

            @pl.when(place[0] == z)
            def _(plan=plan, which=which):
                for far in range(2):
                    for h, (part, base) in enumerate(plan):
                        take = base + (2 * which + far) * modes
                        at = (4 * far + h) * modes
                        wide[:, :, at : at + modes] = part[:, :, take : take + modes].astype(
                            jnp.float32
                        )

        grid[...] = jnp.transpose(wide[...], (1, 0, 2))


def assemble(place, parts, thirds, modes, rows):
    owners = parts[0].shape[0]
    out = jax.ShapeDtypeStruct((rows, owners, 8 * modes), jnp.float32)
    group, tall = min(owners, 8), min(rows, TALL)
    block = pl.BlockSpec((tall, group, 8 * modes), lambda d, r, place: (r, d, 0))
    return pl.pallas_call(
        functools.partial(assemble_kernel, modes),
        out_shape=[out, out],
        grid_spec=pltpu.PrefetchScalarGridSpec(
            num_scalar_prefetch=1,
            grid=(owners // group, pl.cdiv(rows, tall)),
            in_specs=[
                pl.BlockSpec((group, tall, part.shape[2]), lambda d, r, place: (d, r, 0))
                for part in (*parts, *(thirds if len(thirds) == 1 else ()))
            ]
            + [
                pl.BlockSpec((tall, part.shape[1]), lambda d, r, place: (r, 0))
                for part in (thirds if len(thirds) > 1 else ())
            ],
            out_specs=[block] * 2,
            scratch_shapes=[
                pltpu.VMEM((group, tall, 8 * modes), jnp.float32),
                pltpu.VMEM((group, tall, thirds[0].shape[-1]), thirds[0].dtype),
            ],
        ),
        compiler_params=pltpu.CompilerParams(vmem_limit_bytes=56 * MIB),
        cost_estimate=LIGHT,
    )(place, *parts, *thirds)


def moved(shard, axis, by, sources=None):
    length = lax.axis_size(axis)
    sources = range(length) if sources is None else sources
    pairs = [(i, i + by) for i in sources if 0 <= i + by < length]
    return lax.ppermute(shard, axis, pairs)


def to_owners(part, modes):
    count, _, cols = part.shape
    owners = lax.axis_size("sub")
    if owners != count:
        part = part[:, :modes].reshape(owners, count * modes // owners, cols)
    return lax.all_to_all(part, "sub", split_axis=0, concat_axis=0, tiled=True)


def sent_in(phi_packed):
    last = lax.axis_size("grp") - 1
    return moved(phi_packed, "grp", 1, [0]), moved(phi_packed, "grp", -1, [last])


def sent_back(part):
    last = lax.axis_size("grp") - 1
    return lax.ppermute(part, "grp", [(1, 0), (last - 1, last)])


def sent_to_owners(parts):
    last, owners = lax.axis_size("grp") - 1, lax.axis_size("sub")
    moved_to = []
    for k, part in enumerate(parts):
        pairs = []
        for source, target in ((1, 0), (last - 1, last)):
            for sub in range(owners):
                pairs.append((sub * (last + 1) + source, (sub ^ k) * (last + 1) + target))
        moved_to.append(lax.ppermute(part, ("sub", "grp"), pairs))
    return moved_to


def both_ways(left, right):
    return moved(left, "grp", 1), moved(right, "grp", -1)


def main_path(at, lists, ints, phi, psi, border, blocks):
    meta, phi_meta, places, beside = lists
    modes = phi.shape[1]
    hold = lax.optimization_barrier

    own = pack(at, 0, ROOM, meta, psi, border)
    one = both_ways(own, own)
    own, phi, phi_meta = hold((own, phi, phi_meta))
    coupling = couple(at, ROOM, meta, *ints, [phi], *blocks)
    phi_in = sent_in(pack(at, 0, PHI_ROOM, phi_meta, phi))
    one, coupling, beside = hold((one, coupling, beside))
    last = lax.axis_size("grp") - 1
    two = (
        moved(one[0], "grp", 1, range(1, last)),
        moved(one[1], "grp", -1, range(last - 1, 0, -1)),
    )
    (near,) = project(at, meta, [coupling], [(own,), (one[0],), (one[1],)])
    near = to_owners(near, modes)
    end = couple_end(at, meta, ints, places, phi_in, blocks)
    two, near, end = hold((two, near, end))
    direct = lax.axis_size("sub") == phi.shape[0]
    second, *third = project(at, meta, [coupling, end], [two], spread=direct)
    third = sent_to_owners(third) if direct else [sent_back(third[0])]
    second = to_owners(second, modes)
    if not direct:
        third, second, near = hold((third, second, near))
        third = [to_owners(third[0], modes)]
    place = jnp.stack([lax.axis_index("grp"), lax.axis_index("sub")]).astype(jnp.int32)
    rows = phi.shape[0] * modes // lax.axis_size("sub")
    return assemble(place, (near, second), third, modes, rows), two, beside


def without(at, meta, by, room):
    kept = jnp.concatenate([meta[: at.start], jnp.full((at.start,), at.blocks_per, jnp.int32)])
    order = lax.dynamic_slice_in_dim(kept, by, at.start, 0)
    return jnp.concatenate([order, jnp.clip(meta[at.start :] - by, 0, room)])


def columns(part, modes, rows, groups):
    part = part[:, :rows, : groups * 4 * modes].astype(jnp.float32)
    part = part.reshape(*part.shape[:2], groups, 2, 2, modes).transpose(3, 1, 0, 4, 2, 5)
    return part.reshape(2, *part.shape[1:3], 2 * groups * modes)


def add_kernel(old, new, out):
    out[...] = old[...] + new[...]


def added(old, new):
    rows, owners, cols = old.shape
    block = pl.BlockSpec((rows, min(owners, 8), cols), lambda d: (0, d, 0))
    return pl.pallas_call(
        add_kernel,
        out_shape=jax.ShapeDtypeStruct(old.shape, old.dtype),
        grid=(owners // min(owners, 8),),
        in_specs=[block, block],
        out_specs=block,
        input_output_aliases={0: 0},
        compiler_params=pltpu.CompilerParams(vmem_limit_bytes=32 * MIB),
    )(old, new)


def per_device(phi, psi, k_blocks, m_blocks, block_row, block_col, live):
    count, modes, width = phi.shape
    at = Meta(count, k_blocks.shape[1], width // EDGE)
    blocks = (k_blocks, m_blocks)
    ints = (live, block_row, block_col)
    border = moved(psi[count - 1], "sub", 1)
    (whole,) = listed(at, 0, block_col, live)
    phi_whole, places = listed(at, 1, block_row, live, with_places=True)
    total = at.start + count + 1
    most = lax.pmax(jnp.stack([whole[total], phi_whole[total]]), "sub")
    over = jnp.maximum(most - jnp.asarray([ROOM, PHI_ROOM], jnp.int32), 0)
    each = jnp.asarray([MORE, PHI_ROOM], jnp.int32)
    trips = jnp.max((over + each - 1) // each)
    meta = jnp.concatenate([whole[: at.start], jnp.minimum(whole[at.start :], ROOM)])
    lists = (meta, phi_whole, places, trips)
    grids, far, trips = main_path(at, lists, ints, phi, psi, border, blocks)

    def turned(whole):
        return whole.transpose(1, 0, 2)

    def more(state):
        n, phi, psi, far, before = state[0], state[1], state[2], state[3], state[4:]
        phi, psi, far = lax.optimization_barrier((phi, psi, far))
        phi, psi = turned(phi), turned(psi)

        rest = without(at, whole, ROOM + n * MORE, MORE)
        packed = pack(at, 0, MORE, rest, psi, border)
        packed = jnp.stack([packed] * lax.axis_size("grp"))
        packed = lax.all_to_all(packed, "grp", split_axis=0, concat_axis=0, tiled=True)
        coupling = couple(at, MORE, rest, *ints, [phi], *blocks)
        shards = [(packed[h],) for h in range(packed.shape[0])]
        part = to_owners(project(at, rest, [coupling], shards)[0], modes)
        after = columns(part, modes, grids[0].shape[0], len(shards))

        skipped = (n + 1) * PHI_ROOM
        rest = without(at, phi_whole, skipped, PHI_ROOM)
        phi_in = sent_in(pack(at, 0, PHI_ROOM, rest, phi))
        end = couple_end(at, meta, ints, places - skipped, phi_in, blocks)
        (part,) = project(at, meta, [end], [far])
        part = columns(to_owners(sent_back(part), modes), modes, grids[0].shape[0], 1)
        place, zero = lax.axis_index("grp"), jnp.zeros_like(part[..., :modes])
        last = lax.axis_size("grp") - 1
        ends = []
        for low in (0, modes):
            one = part[..., low : low + modes]
            for h in range(last + 1):
                wanted = ((place == 0) & (h == last)) | ((place == last) & (h == 0))
                ends.append(jnp.where(wanted, one, zero))
        after = after + jnp.concatenate(ends, axis=-1)
        return (n + 1, *state[1:4], *(added(old, new) for old, new in zip(before, after)))

    state = (jnp.int32(0), turned(phi), turned(psi), far, *grids)
    state = lax.while_loop(lambda state: state[0] < trips, more, state)
    return tuple(turned(grid)[None, None] for grid in state[4:])


def solution(mesh):
    placed = (
        P("sub", "grp", None),
        P("sub", "grp", None),
        P("sub", None, None, None),
        P("sub", None, None, None),
        P("sub", None),
        P("sub", None),
        P("sub"),
    )
    return jax.shard_map(
        per_device,
        mesh=mesh,
        in_specs=placed,
        out_specs=(P("sub", "grp", None, None, None), P("sub", "grp", None, None, None)),
        check_vma=False,
    )
```

```python
import functools

import jax
import jax.numpy as jnp
from jax import lax
from jax.experimental import pallas as pl
from jax.experimental.pallas import tpu as pltpu
from jax.sharding import PartitionSpec as P

EDGE = 128
ROWS = 112
SLOTS = 8
BITE = 4
ROOM = 94
PHI_ROOM = 92
MORE = 16
MIB = 1 << 20
LIGHT = pl.CostEstimate(flops=1, bytes_accessed=1, transcendentals=0)
HEAVY = pl.CostEstimate(flops=25_000_000_000, bytes_accessed=1, transcendentals=0)


def up_to(limit, body, unroll=1):
    lax.fori_loop(0, limit, lambda n, _: (body(n), 0)[1], 0, unroll=unroll)


def by_four(limit, body):
    def four(step):
        for k in range(4):
            body(jnp.minimum(step * 4 + k, limit - 1))

    up_to((limit + 3) // 4, four)


def lanes(block, count=1):
    return pl.ds(pl.multiple_of(block * EDGE, EDGE), count * EDGE)


class Meta:
    def __init__(self, count, slots, blocks_per):
        self.count, self.slots, self.blocks_per = count, slots, blocks_per
        self.keys = (count + 1) * blocks_per
        self.order = 0
        self.start = self.keys + max(ROOM + MORE, 2 * PHI_ROOM)
        self.size = self.start + count + 2


def list_kernel(at, shift, live, block, meta, *refs):
    (*places, flags) = refs

    def clear(n):
        flags[n] = 0

    up_to(at.keys, clear, unroll=16)
    for i in range(at.count):

        def mark(n, i=i):
            flags[block[i, n] + (i + shift) * at.blocks_per] = 1

        up_to(live[i], mark)

    def place(key, taken):
        needed = flags[key]
        meta[at.order + taken] = key
        flags[key] = taken
        return taken + needed

    taken = 0
    for side in range(at.count + 1):
        meta[at.start + side] = taken
        taken = lax.fori_loop(
            side * at.blocks_per, (side + 1) * at.blocks_per, place, taken, unroll=at.blocks_per
        )
    meta[at.start + at.count + 1] = taken

    for found in places:
        for i in range(at.count):

            def find(n, i=i, found=found):
                found[i, n] = flags[block[i, n] + (i + shift) * at.blocks_per]

            up_to(live[i], find)


def listed(at, shift, block, live, with_places=False):
    out = [jax.ShapeDtypeStruct((at.size,), jnp.int32)]
    if with_places:
        out.append(jax.ShapeDtypeStruct(block.shape, jnp.int32))
    return pl.pallas_call(
        functools.partial(list_kernel, at, shift),
        out_shape=out,
        in_specs=[pl.BlockSpec(memory_space=pltpu.SMEM)] * 2,
        out_specs=[pl.BlockSpec(memory_space=pltpu.SMEM)] * len(out),
        scratch_shapes=[pltpu.SMEM((at.keys,), jnp.int32)],
        cost_estimate=LIGHT,
    )(live, block)


def pack_kernel(at, first, room, meta, *refs):
    borders, psi, out = refs[:-2], refs[-2], refs[-1]
    split = jnp.clip(meta[at.start + 1] - first, 0, room)
    end = jnp.clip(meta[at.start + at.count + 1] - first, 0, room)

    def from_border(c):
        for border in borders:
            out[:, lanes(c)] = border[:, lanes(meta[at.order + first + c])]

    def from_psi(c):
        key = meta[at.order + first + c]
        out[:, lanes(c)] = psi[key // at.blocks_per - 1, :, lanes(key % at.blocks_per)]

    def from_none(c):
        out[:, lanes(c)] = jnp.zeros((out.shape[0], EDGE), out.dtype)

    up_to(split, from_border)
    up_to(end - split, lambda c: from_psi(split + c))
    up_to(room - end, lambda c: from_none(end + c))


def pack(at, first, room, meta, psi, *borders):
    return pl.pallas_call(
        functools.partial(pack_kernel, at, first, room),
        out_shape=jax.ShapeDtypeStruct((psi.shape[1], room * EDGE), psi.dtype),
        in_specs=[pl.BlockSpec(memory_space=pltpu.SMEM)]
        + [pl.BlockSpec(memory_space=pltpu.VMEM)] * (1 + len(borders)),
        out_specs=pl.BlockSpec(memory_space=pltpu.VMEM),
        compiler_params=pltpu.CompilerParams(vmem_limit_bytes=8 * MIB),
        cost_estimate=LIGHT,
    )(meta, *borders, psi)


def coupling_kernel(at, room, many, meta, live, row, col, *refs):
    phis, (k_blocks, m_blocks, out, total) = refs[:many], refs[many:]
    i = pl.program_id(0)
    couple_one(at, room, i, meta, live, row, col, phis, k_blocks, m_blocks, out, total)


def couple_one(at, room, i, meta, live, row, col, phis, k_blocks, m_blocks, out, total):
    modes, blocks = phis[0].shape[1], phis[0].shape[2] // EDGE
    here, middle, end = (meta[at.start + i + n] for n in range(3))
    first = at.blocks_per * i

    def clear(n):
        total[meta[at.order + here + n] - first] = jnp.zeros(total.shape[1:], total.dtype)

    by_four(end - here, clear)

    def add_slots(step):
        terms = []
        for n in range(SLOTS):
            slot = jnp.minimum(step * SLOTS + n, at.slots - 1)
            where = row[i, slot]
            here = (step * SLOTS + n < live[i]) & (where >= 0) & (where < blocks)
            which = lanes(jnp.clip(where, 0, blocks - 1))
            picked = sum([phi[0, :, which] for phi in phis[1:]], phis[0][0, :, which])
            both = jnp.concatenate([k_blocks[0, slot], m_blocks[0, slot]], axis=1)
            to = jnp.where(here, col[i, slot], 2 * at.blocks_per)
            terms.append((to, jnp.dot(picked, both, preferred_element_type=jnp.float32)))
        for to, term in terms:
            total[to] += term

    up_to((live[i] + SLOTS - 1) // SLOTS, add_slots)

    def put(flavour, c):
        done = total[meta[at.order + c] - first].astype(out.dtype)
        out[flavour * ROWS : flavour * ROWS + modes, lanes(c)] = done[:, :EDGE]
        out[(flavour + 1) * ROWS : (flavour + 1) * ROWS + modes, lanes(c)] = done[:, EDGE:]

    def blank(top, c):
        out[top : top + 2 * ROWS, lanes(c)] = jnp.zeros((2 * ROWS, EDGE), out.dtype)

    by_four(middle - here, lambda n: put(2, here + n))
    by_four(end - middle, lambda n: put(0, middle + n))

    @pl.when(i == 0)
    def _():
        up_to(middle, lambda n: blank(0, n))

    @pl.when(i == at.count - 1)
    def _():
        up_to(room - middle, lambda n: blank(2 * ROWS, middle + n))
        up_to(room - end, lambda n: blank(0, end + n))


def couple(at, room, meta, live, row, col, phis, k_blocks, m_blocks, cost=LIGHT):
    _, modes, width = phis[0].shape
    count, slots = k_blocks.shape[:2]
    return pl.pallas_call(
        functools.partial(coupling_kernel, at, room, len(phis)),
        out_shape=jax.ShapeDtypeStruct((4 * ROWS, room * EDGE), phis[0].dtype),
        grid_spec=pltpu.PrefetchScalarGridSpec(
            num_scalar_prefetch=4,
            grid=(count,),
            in_specs=[
                pl.BlockSpec(
                    (1, modes, width), lambda i, *_, phi=phi: (0 if phi.shape[0] == 1 else i, 0, 0)
                )
                for phi in phis
            ]
            + [pl.BlockSpec((1, slots, EDGE, EDGE), lambda i, *_: (i, 0, 0, 0))] * 2,
            out_specs=pl.BlockSpec(
                (4 * ROWS, room * EDGE), lambda i, *_: (0, 0), pipeline_mode=pl.Buffered(1)
            ),
            scratch_shapes=[pltpu.VMEM((2 * at.blocks_per + 1, modes, 2 * EDGE), jnp.float32)],
        ),
        compiler_params=pltpu.CompilerParams(vmem_limit_bytes=56 * MIB),
        cost_estimate=cost,
    )(meta, live, row, col, *phis, k_blocks, m_blocks)


def sum_blocks(at, meta, bounds, couplings, shard, groups, right, totals):
    low, high = bounds
    modes = shard.shape[1]

    def on_side(side):
        begin = jnp.maximum(meta[at.start + side], low)
        end = jnp.minimum(meta[at.start + side + 1], high)

        def bite(n):
            want = begin + n * BITE
            first = jnp.minimum(want, high - BITE)
            lane = lax.broadcasted_iota(jnp.int32, (modes, BITE * EDGE), 1) + first * EDGE
            inside = (lane >= want * EDGE) & (lane < end * EDGE)
            for g, group in enumerate(groups):
                part = shard[group[0], :, lanes(first, BITE)]
                for other in group[1:]:
                    part = part + shard[other, :, lanes(first, BITE)]
                part = jnp.where(inside, part, jnp.zeros_like(part))
                right[g * EDGE : g * EDGE + modes, :] = part
            for coupling, total in zip(couplings, totals):
                total[side] += lax.dot_general(
                    coupling[:, lanes(first, BITE)],
                    right[...],
                    (((1,), (1,)), ((), ())),
                    preferred_element_type=jnp.float32,
                )

        up_to(jnp.maximum(end - begin + BITE - 1, 0) // BITE, bite)

    up_to(at.count + 1, on_side)


def put_products(at, groups, modes, total, out):
    for side in range(at.count + 1):
        for g in range(len(groups)):
            for flavour, (sub, part) in enumerate(
                ((side - 1, 1), (side - 1, 3), (side, 0), (side, 2))
            ):
                if 0 <= sub < at.count:
                    top, to = flavour * ROWS, (g * 4 + part) * modes
                    one = total[side, top : top + modes, g * EDGE : g * EDGE + modes]
                    out[sub, :modes, to : to + modes] = one.astype(out.dtype)


def grouped(sets):
    groups, taken = [], 0
    for size in sets:
        groups.append(range(taken, taken + size))
        taken += size
    return groups


def put_spread(at, modes, me, total, outs):
    for k, out in enumerate(outs):
        sub = jnp.bitwise_xor(me, k)
        for part, (side, flavour) in enumerate(((sub, 2), (sub + 1, 0), (sub, 3), (sub + 1, 1))):
            one = total[side, flavour * ROWS : flavour * ROWS + modes, :modes]
            out[:modes, part * modes : (part + 1) * modes] = one.astype(out.dtype)


def project_kernel(at, room, sets, many, spread, meta, me, *refs):
    couplings, refs = refs[:many], refs[many:]
    shards, refs = refs[: sum(sets)], refs[sum(sets) :]
    pieces = at.count if spread else 0
    outs, spreads, refs = refs[:many], refs[many - 1 : many - 1 + pieces], refs[many + max(pieces - 1, 0) :]
    helds, totals, (shard, right, held_done, shard_done) = refs[:many], refs[many : 2 * many], refs[2 * many :]
    parts = [(0, room // 2), (room // 2, room)]
    coming = [[], []]
    for k, one in enumerate(shards):
        coming[0].append(pltpu.make_async_copy(one, shard.at[k], shard_done.at[k]))
    for n, (low, high) in enumerate(parts):
        to = pl.ds(low * EDGE, (high - low) * EDGE)
        for k, (coupling, held) in enumerate(zip(couplings, helds)):
            coming[n].append(
                pltpu.make_async_copy(coupling.at[:, to], held.at[:, to], held_done.at[2 * k + n])
            )
    for copy in coming[0] + coming[1]:
        copy.start()
    right[...] = jnp.zeros(right.shape, right.dtype)
    for total in totals:
        total[...] = jnp.zeros(total.shape, total.dtype)
    for bounds, here in zip(parts, coming):
        for copy in here:
            copy.wait()
        sum_blocks(at, meta, bounds, helds, shard, grouped(sets), right, totals)
    for n, (total, out) in enumerate(zip(totals, outs)):
        if spread and n == many - 1:
            put_spread(at, shard.shape[1], me[0], total, spreads)
        else:
            put_products(at, grouped(sets), shard.shape[1], total, out)


def project(at, meta, couplings, groups, spread=False):
    flat = [shard for group in groups for shard in group]
    modes, held = flat[0].shape[0], couplings[0]
    sets = tuple(len(group) for group in groups)
    n, many, room = len(groups), len(couplings), held.shape[1] // EDGE
    wide = -(-n * 4 * modes // EDGE) * EDGE
    tall = -(-modes // 8) * 8
    out = [jax.ShapeDtypeStruct((at.count, tall, wide), held.dtype)] * many
    if spread:
        out = out[:-1] + [jax.ShapeDtypeStruct((tall, wide), held.dtype)] * at.count
    me = lax.axis_index("sub").astype(jnp.int32)[None]
    return pl.pallas_call(
        functools.partial(project_kernel, at, room, sets, many, spread),
        out_shape=out,
        in_specs=[pl.BlockSpec(memory_space=pltpu.SMEM)] * 2
        + [pl.BlockSpec(memory_space=pltpu.HBM)] * (many + len(flat)),
        out_specs=[pl.BlockSpec(memory_space=pltpu.VMEM)] * len(out),
        scratch_shapes=[pltpu.VMEM(held.shape, held.dtype)] * many
        + [pltpu.VMEM((at.count + 1, 4 * ROWS, n * EDGE), jnp.float32)] * many
        + [
            pltpu.VMEM((len(flat), modes, held.shape[1]), held.dtype),
            pltpu.VMEM((n * EDGE, BITE * EDGE), held.dtype),
            pltpu.SemaphoreType.DMA((2 * many,)),
            pltpu.SemaphoreType.DMA((len(flat),)),
        ],
        compiler_params=pltpu.CompilerParams(vmem_limit_bytes=56 * MIB),
        cost_estimate=LIGHT,
    )(meta, me, *couplings, *flat)


def couple_end(at, meta, ints, places, phi_in, blocks):
    live, _, col = ints
    phis = [one[None] for one in phi_in]
    return couple(at, ROOM, meta, live, places, col, phis, *blocks, cost=HEAVY)


def assemble_kernel(modes, place, near, second, *refs):
    rows = refs[-2].shape[1]
    thirds, (grid_k, grid_m, wide, sorted_third) = refs[:-4], refs[-4:]
    third = thirds[0]
    if len(thirds) > 1:
        third = sorted_third
        for k, one in enumerate(thirds):
            third[jnp.bitwise_xor(place[1], k)] = one[...]
    own, left, right = ((near, g * 4 * modes) for g in range(3))
    second, third = (second, 0), (third, 0)
    plans = (
        (own, right, second, third),
        (left, own, right, second),
        (second, left, own, right),
        (third, second, left, own),
    )
    for which, grid in enumerate((grid_k, grid_m)):
        for z, plan in enumerate(plans):

            @pl.when(place[0] == z)
            def _(plan=plan, which=which):
                for far in range(2):
                    for h, (part, base) in enumerate(plan):
                        take = base + (2 * which + far) * modes
                        at = (4 * far + h) * modes
                        wide[:, :, at : at + modes] = part[:, :rows, take : take + modes].astype(
                            jnp.float32
                        )

        grid[...] = jnp.transpose(wide[...], (1, 0, 2))


def assemble(place, parts, thirds, modes, rows):
    owners = parts[0].shape[0]
    out = jax.ShapeDtypeStruct((rows, owners, 8 * modes), jnp.float32)
    group = min(owners, 8)
    block = pl.BlockSpec((rows, group, 8 * modes), lambda d, place: (0, d, 0))

    def taken(part):
        if len(part.shape) == 2:
            return pl.BlockSpec(part.shape, lambda d, place: (0, 0))
        return pl.BlockSpec((group, *part.shape[1:]), lambda d, place: (d, 0, 0))

    return pl.pallas_call(
        functools.partial(assemble_kernel, modes),
        out_shape=[out, out],
        grid_spec=pltpu.PrefetchScalarGridSpec(
            num_scalar_prefetch=1,
            grid=(owners // group,),
            in_specs=[taken(part) for part in (*parts, *thirds)],
            out_specs=[block] * 2,
            scratch_shapes=[
                pltpu.VMEM((group, rows, 8 * modes), jnp.float32),
                pltpu.VMEM((group, *thirds[0].shape[-2:]), thirds[0].dtype),
            ],
        ),
        compiler_params=pltpu.CompilerParams(vmem_limit_bytes=56 * MIB),
        cost_estimate=LIGHT,
    )(place, *parts, *thirds)


def moved(shard, axis, by, sources=None):
    length = lax.axis_size(axis)
    sources = range(length) if sources is None else sources
    pairs = [(i, i + by) for i in sources if 0 <= i + by < length]
    return lax.ppermute(shard, axis, pairs)


def to_owners(part, modes):
    count, _, cols = part.shape
    owners = lax.axis_size("sub")
    if owners != count:
        part = part[:, :modes].reshape(owners, count * modes // owners, cols)
    return lax.all_to_all(part, "sub", split_axis=0, concat_axis=0, tiled=True)


def sent_in(phi_packed):
    last = lax.axis_size("grp") - 1
    return moved(phi_packed, "grp", 1, [0]), moved(phi_packed, "grp", -1, [last])


def sent_back(part):
    last = lax.axis_size("grp") - 1
    return lax.ppermute(part, "grp", [(1, 0), (last - 1, last)])


def sent_to_owners(parts):
    last, owners = lax.axis_size("grp") - 1, lax.axis_size("sub")
    moved_to = []
    for k, part in enumerate(parts):
        pairs = []
        for source, target in ((1, 0), (last - 1, last)):
            for sub in range(owners):
                pairs.append((sub * (last + 1) + source, (sub ^ k) * (last + 1) + target))
        moved_to.append(lax.ppermute(part, ("sub", "grp"), pairs))
    return moved_to


def both_ways(left, right):
    return moved(left, "grp", 1), moved(right, "grp", -1)


def main_path(at, lists, ints, phi, psi, border, blocks):
    meta, phi_meta, places, beside = lists
    modes = phi.shape[1]
    hold = lax.optimization_barrier

    own = pack(at, 0, ROOM, meta, psi, border)
    one = both_ways(own, own)
    own, phi, phi_meta = hold((own, phi, phi_meta))
    coupling = couple(at, ROOM, meta, *ints, [phi], *blocks)
    phi_in = sent_in(pack(at, 0, PHI_ROOM, phi_meta, phi))
    one, coupling, beside = hold((one, coupling, beside))
    last = lax.axis_size("grp") - 1
    two = (
        moved(one[0], "grp", 1, range(1, last)),
        moved(one[1], "grp", -1, range(last - 1, 0, -1)),
    )
    (near,) = project(at, meta, [coupling], [(own,), (one[0],), (one[1],)])
    near = to_owners(near, modes)
    end = couple_end(at, meta, ints, places, phi_in, blocks)
    two, near, end = hold((two, near, end))
    direct = lax.axis_size("sub") == phi.shape[0]
    second, *third = project(at, meta, [coupling, end], [two], spread=direct)
    third = sent_to_owners(third) if direct else [sent_back(third[0])]
    second = to_owners(second, modes)
    if not direct:
        third, second, near = hold((third, second, near))
        third = [to_owners(third[0], modes)]
    place = jnp.stack([lax.axis_index("grp"), lax.axis_index("sub")]).astype(jnp.int32)
    rows = phi.shape[0] * modes // lax.axis_size("sub")
    return assemble(place, (near, second), third, modes, rows), two, beside, phi


def without(at, meta, by, room):
    kept = jnp.concatenate([meta[: at.start], jnp.full((at.start,), at.blocks_per, jnp.int32)])
    order = lax.dynamic_slice_in_dim(kept, by, at.start, 0)
    return jnp.concatenate([order, jnp.clip(meta[at.start :] - by, 0, room)])


def columns(part, modes, rows, groups):
    part = part[:, :rows, : groups * 4 * modes].astype(jnp.float32)
    part = part.reshape(*part.shape[:2], groups, 2, 2, modes).transpose(3, 1, 0, 4, 2, 5)
    return part.reshape(2, *part.shape[1:3], 2 * groups * modes)


def add_kernel(old, new, out):
    out[...] = old[...] + new[...]


def added(old, new):
    rows, owners, cols = old.shape
    block = pl.BlockSpec((rows, min(owners, 8), cols), lambda d: (0, d, 0))
    return pl.pallas_call(
        add_kernel,
        out_shape=jax.ShapeDtypeStruct(old.shape, old.dtype),
        grid=(owners // min(owners, 8),),
        in_specs=[block, block],
        out_specs=block,
        input_output_aliases={0: 0},
        compiler_params=pltpu.CompilerParams(vmem_limit_bytes=32 * MIB),
    )(old, new)


def per_device(phi, psi, k_blocks, m_blocks, block_row, block_col, live):
    count, modes, width = phi.shape
    at = Meta(count, k_blocks.shape[1], width // EDGE)
    blocks = (k_blocks, m_blocks)
    ints = (live, block_row, block_col)
    border = moved(psi[count - 1], "sub", 1)
    (whole,) = listed(at, 0, block_col, live)
    phi_whole, places = listed(at, 1, block_row, live, with_places=True)
    total = at.start + count + 1
    most = lax.pmax(jnp.stack([whole[total], phi_whole[total]]), "sub")
    over = jnp.maximum(most - jnp.asarray([ROOM, PHI_ROOM], jnp.int32), 0)
    each = jnp.asarray([MORE, PHI_ROOM], jnp.int32)
    trips = jnp.max((over + each - 1) // each)
    meta = jnp.concatenate([whole[: at.start], jnp.minimum(whole[at.start :], ROOM)])
    lists = (meta, phi_whole, places, trips)
    grids, far, trips, phi = main_path(at, lists, ints, phi, psi, border, blocks)

    def turned(whole):
        return whole.transpose(1, 0, 2)

    def more(state):
        n, phi, psi, far, before = state[0], state[1], state[2], state[3], state[4:]
        phi, psi, far = lax.optimization_barrier((phi, psi, far))
        phi, psi = turned(phi), turned(psi)

        rest = without(at, whole, ROOM + n * MORE, MORE)
        packed = pack(at, 0, MORE, rest, psi, border)
        packed = jnp.stack([packed] * lax.axis_size("grp"))
        packed = lax.all_to_all(packed, "grp", split_axis=0, concat_axis=0, tiled=True)
        coupling = couple(at, MORE, rest, *ints, [phi], *blocks)
        shards = [(packed[h],) for h in range(packed.shape[0])]
        part = to_owners(project(at, rest, [coupling], shards)[0], modes)
        after = columns(part, modes, grids[0].shape[0], len(shards))

        skipped = (n + 1) * PHI_ROOM
        rest = without(at, phi_whole, skipped, PHI_ROOM)
        phi_in = sent_in(pack(at, 0, PHI_ROOM, rest, phi))
        end = couple_end(at, meta, ints, places - skipped, phi_in, blocks)
        (part,) = project(at, meta, [end], [far])
        part = columns(to_owners(sent_back(part), modes), modes, grids[0].shape[0], 1)
        place, zero = lax.axis_index("grp"), jnp.zeros_like(part[..., :modes])
        last = lax.axis_size("grp") - 1
        ends = []
        for low in (0, modes):
            one = part[..., low : low + modes]
            for h in range(last + 1):
                wanted = ((place == 0) & (h == last)) | ((place == last) & (h == 0))
                ends.append(jnp.where(wanted, one, zero))
        after = after + jnp.concatenate(ends, axis=-1)
        return (n + 1, *state[1:4], *(added(old, new) for old, new in zip(before, after)))

    state = (jnp.int32(0), turned(phi), turned(psi), far, *grids)
    state = lax.while_loop(lambda state: state[0] < trips, more, state)
    return tuple(turned(grid)[None, None] for grid in state[4:])


def solution(mesh):
    placed = (
        P("sub", "grp", None),
        P("sub", "grp", None),
        P("sub", None, None, None),
        P("sub", None, None, None),
        P("sub", None),
        P("sub", None),
        P("sub"),
    )
    return jax.shard_map(
        per_device,
        mesh=mesh,
        in_specs=placed,
        out_specs=(P("sub", "grp", None, None, None), P("sub", "grp", None, None, None)),
        check_vma=False,
    )
```

```python
import functools

import jax
import jax.numpy as jnp
from jax import lax
from jax.experimental import pallas as pl
from jax.experimental.pallas import tpu as pltpu
from jax.sharding import PartitionSpec as P

EDGE = 128
ROWS = 112
SLOTS = 8
BITE = 4
ROOM = 94
PHI_ROOM = 90
MORE = 16
MIB = 1 << 20
LIGHT = pl.CostEstimate(flops=1, bytes_accessed=1, transcendentals=0)
HEAVY = pl.CostEstimate(flops=25_000_000_000, bytes_accessed=1, transcendentals=0)


def up_to(limit, body, unroll=1):
    lax.fori_loop(0, limit, lambda n, _: (body(n), 0)[1], 0, unroll=unroll)


def by_four(limit, body):
    def four(step):
        for k in range(4):
            body(jnp.minimum(step * 4 + k, limit - 1))

    up_to((limit + 3) // 4, four)


def lanes(block, count=1):
    return pl.ds(pl.multiple_of(block * EDGE, EDGE), count * EDGE)


class Meta:
    def __init__(self, count, slots, blocks_per):
        self.count, self.slots, self.blocks_per = count, slots, blocks_per
        self.keys = (count + 1) * blocks_per
        self.order = 0
        self.start = self.keys + max(ROOM + MORE, 2 * PHI_ROOM)
        self.size = self.start + count + 2


def list_kernel(at, shift, live, block, meta, *refs):
    (*places, flags) = refs

    def clear(n):
        flags[n] = 0

    up_to(at.keys, clear, unroll=16)
    for i in range(at.count):

        def mark(n, i=i):
            flags[block[i, n] + (i + shift) * at.blocks_per] = 1

        up_to(live[i], mark)

    def place(key, taken):
        needed = flags[key]
        meta[at.order + taken] = key
        flags[key] = taken
        return taken + needed

    taken = 0
    for side in range(at.count + 1):
        meta[at.start + side] = taken
        taken = lax.fori_loop(
            side * at.blocks_per, (side + 1) * at.blocks_per, place, taken, unroll=at.blocks_per
        )
    meta[at.start + at.count + 1] = taken

    for found in places:
        for i in range(at.count):

            def find(n, i=i, found=found):
                found[i, n] = flags[block[i, n] + (i + shift) * at.blocks_per]

            up_to(live[i], find)


def listed(at, shift, block, live, with_places=False):
    out = [jax.ShapeDtypeStruct((at.size,), jnp.int32)]
    if with_places:
        out.append(jax.ShapeDtypeStruct(block.shape, jnp.int32))
    return pl.pallas_call(
        functools.partial(list_kernel, at, shift),
        out_shape=out,
        in_specs=[pl.BlockSpec(memory_space=pltpu.SMEM)] * 2,
        out_specs=[pl.BlockSpec(memory_space=pltpu.SMEM)] * len(out),
        scratch_shapes=[pltpu.SMEM((at.keys,), jnp.int32)],
        cost_estimate=LIGHT,
    )(live, block)


def pack_kernel(at, first, room, meta, *refs):
    borders, psi, out = refs[:-2], refs[-2], refs[-1]
    split = jnp.clip(meta[at.start + 1] - first, 0, room)
    end = jnp.clip(meta[at.start + at.count + 1] - first, 0, room)

    def from_border(c):
        for border in borders:
            out[:, lanes(c)] = border[:, lanes(meta[at.order + first + c])]

    def from_psi(c):
        key = meta[at.order + first + c]
        out[:, lanes(c)] = psi[key // at.blocks_per - 1, :, lanes(key % at.blocks_per)]

    def from_none(c):
        out[:, lanes(c)] = jnp.zeros((out.shape[0], EDGE), out.dtype)

    up_to(split, from_border)
    up_to(end - split, lambda c: from_psi(split + c))
    up_to(room - end, lambda c: from_none(end + c))


def pack(at, first, room, meta, psi, *borders):
    return pl.pallas_call(
        functools.partial(pack_kernel, at, first, room),
        out_shape=jax.ShapeDtypeStruct((psi.shape[1], room * EDGE), psi.dtype),
        in_specs=[pl.BlockSpec(memory_space=pltpu.SMEM)]
        + [pl.BlockSpec(memory_space=pltpu.VMEM)] * (1 + len(borders)),
        out_specs=pl.BlockSpec(memory_space=pltpu.VMEM),
        compiler_params=pltpu.CompilerParams(vmem_limit_bytes=8 * MIB),
        cost_estimate=LIGHT,
    )(meta, *borders, psi)


def coupling_kernel(at, room, many, meta, live, row, col, *refs):
    phis, (k_blocks, m_blocks, out, total) = refs[:many], refs[many:]
    i = pl.program_id(0)
    couple_one(at, room, i, meta, live, row, col, phis, k_blocks, m_blocks, out, total)


def couple_one(at, room, i, meta, live, row, col, phis, k_blocks, m_blocks, out, total):
    modes, blocks = phis[0].shape[1], phis[0].shape[2] // EDGE
    here, middle, end = (meta[at.start + i + n] for n in range(3))
    first = at.blocks_per * i

    def clear(n):
        total[meta[at.order + here + n] - first] = jnp.zeros(total.shape[1:], total.dtype)

    by_four(end - here, clear)

    def add_slots(step):
        terms = []
        for n in range(SLOTS):
            slot = jnp.minimum(step * SLOTS + n, at.slots - 1)
            where = row[i, slot]
            here = (step * SLOTS + n < live[i]) & (where >= 0) & (where < blocks)
            which = lanes(jnp.clip(where, 0, blocks - 1))
            picked = sum([phi[0, :, which] for phi in phis[1:]], phis[0][0, :, which])
            both = jnp.concatenate([k_blocks[0, slot], m_blocks[0, slot]], axis=1)
            to = jnp.where(here, col[i, slot], 2 * at.blocks_per)
            terms.append((to, jnp.dot(picked, both, preferred_element_type=jnp.float32)))
        for to, term in terms:
            total[to] += term

    up_to((live[i] + SLOTS - 1) // SLOTS, add_slots)

    def put(flavour, c):
        done = total[meta[at.order + c] - first].astype(out.dtype)
        out[flavour * ROWS : flavour * ROWS + modes, lanes(c)] = done[:, :EDGE]
        out[(flavour + 1) * ROWS : (flavour + 1) * ROWS + modes, lanes(c)] = done[:, EDGE:]

    def blank(top, c):
        out[top : top + 2 * ROWS, lanes(c)] = jnp.zeros((2 * ROWS, EDGE), out.dtype)

    by_four(middle - here, lambda n: put(2, here + n))
    by_four(end - middle, lambda n: put(0, middle + n))

    @pl.when(i == 0)
    def _():
        up_to(middle, lambda n: blank(0, n))

    @pl.when(i == at.count - 1)
    def _():
        up_to(room - middle, lambda n: blank(2 * ROWS, middle + n))
        up_to(room - end, lambda n: blank(0, end + n))


def couple(at, room, meta, live, row, col, phis, k_blocks, m_blocks, cost=LIGHT):
    _, modes, width = phis[0].shape
    count, slots = k_blocks.shape[:2]
    return pl.pallas_call(
        functools.partial(coupling_kernel, at, room, len(phis)),
        out_shape=jax.ShapeDtypeStruct((4 * ROWS, room * EDGE), phis[0].dtype),
        grid_spec=pltpu.PrefetchScalarGridSpec(
            num_scalar_prefetch=4,
            grid=(count,),
            in_specs=[
                pl.BlockSpec(
                    (1, modes, width), lambda i, *_, phi=phi: (0 if phi.shape[0] == 1 else i, 0, 0)
                )
                for phi in phis
            ]
            + [pl.BlockSpec((1, slots, EDGE, EDGE), lambda i, *_: (i, 0, 0, 0))] * 2,
            out_specs=pl.BlockSpec(
                (4 * ROWS, room * EDGE), lambda i, *_: (0, 0), pipeline_mode=pl.Buffered(1)
            ),
            scratch_shapes=[pltpu.VMEM((2 * at.blocks_per + 1, modes, 2 * EDGE), jnp.float32)],
        ),
        compiler_params=pltpu.CompilerParams(vmem_limit_bytes=56 * MIB),
        cost_estimate=cost,
    )(meta, live, row, col, *phis, k_blocks, m_blocks)


def sum_blocks(at, meta, bounds, couplings, shard, groups, right, totals):
    low, high = bounds
    modes = shard.shape[1]

    def on_side(side):
        begin = jnp.maximum(meta[at.start + side], low)
        end = jnp.minimum(meta[at.start + side + 1], high)

        def bite(n):
            want = begin + n * BITE
            first = jnp.minimum(want, high - BITE)
            lane = lax.broadcasted_iota(jnp.int32, (modes, BITE * EDGE), 1) + first * EDGE
            inside = (lane >= want * EDGE) & (lane < end * EDGE)
            for g, group in enumerate(groups):
                part = shard[group[0], :, lanes(first, BITE)]
                for other in group[1:]:
                    part = part + shard[other, :, lanes(first, BITE)]
                part = jnp.where(inside, part, jnp.zeros_like(part))
                right[g * EDGE : g * EDGE + modes, :] = part
            for coupling, total in zip(couplings, totals):
                total[side] += lax.dot_general(
                    coupling[:, lanes(first, BITE)],
                    right[...],
                    (((1,), (1,)), ((), ())),
                    preferred_element_type=jnp.float32,
                )

        up_to(jnp.maximum(end - begin + BITE - 1, 0) // BITE, bite)

    up_to(at.count + 1, on_side)


def put_products(at, groups, modes, total, out):
    for side in range(at.count + 1):
        for g in range(len(groups)):
            for flavour, (sub, part) in enumerate(
                ((side - 1, 1), (side - 1, 3), (side, 0), (side, 2))
            ):
                if 0 <= sub < at.count:
                    top, to = flavour * ROWS, (g * 4 + part) * modes
                    one = total[side, top : top + modes, g * EDGE : g * EDGE + modes]
                    out[sub, :modes, to : to + modes] = one.astype(out.dtype)


def grouped(sets):
    groups, taken = [], 0
    for size in sets:
        groups.append(range(taken, taken + size))
        taken += size
    return groups


def put_spread(at, modes, me, total, outs):
    for k, out in enumerate(outs):
        sub = jnp.bitwise_xor(me, k)
        for part, (side, flavour) in enumerate(((sub, 2), (sub + 1, 0), (sub, 3), (sub + 1, 1))):
            one = total[side, flavour * ROWS : flavour * ROWS + modes, :modes]
            out[:modes, part * modes : (part + 1) * modes] = one.astype(out.dtype)


def project_kernel(at, room, sets, many, spread, meta, me, *refs):
    couplings, refs = refs[:many], refs[many:]
    shards, refs = refs[: sum(sets)], refs[sum(sets) :]
    pieces = at.count if spread else 0
    outs, spreads, refs = refs[:many], refs[many - 1 : many - 1 + pieces], refs[many + max(pieces - 1, 0) :]
    helds, totals, (shard, right, held_done, shard_done) = refs[:many], refs[many : 2 * many], refs[2 * many :]
    parts = [(0, room // 4), (room // 4, room)]
    coming = [[], []]
    for k, one in enumerate(shards):
        coming[0].append(pltpu.make_async_copy(one, shard.at[k], shard_done.at[k]))
    for n, (low, high) in enumerate(parts):
        to = pl.ds(low * EDGE, (high - low) * EDGE)
        for k, (coupling, held) in enumerate(zip(couplings, helds)):
            coming[n].append(
                pltpu.make_async_copy(coupling.at[:, to], held.at[:, to], held_done.at[2 * k + n])
            )
    for copy in coming[0] + coming[1]:
        copy.start()
    right[...] = jnp.zeros(right.shape, right.dtype)
    for total in totals:
        total[...] = jnp.zeros(total.shape, total.dtype)
    for bounds, here in zip(parts, coming):
        for copy in here:
            copy.wait()
        sum_blocks(at, meta, bounds, helds, shard, grouped(sets), right, totals)
    for n, (total, out) in enumerate(zip(totals, outs)):
        if spread and n == many - 1:
            put_spread(at, shard.shape[1], me[0], total, spreads)
        else:
            put_products(at, grouped(sets), shard.shape[1], total, out)


def project(at, meta, couplings, groups, spread=False):
    flat = [shard for group in groups for shard in group]
    modes, held = flat[0].shape[0], couplings[0]
    sets = tuple(len(group) for group in groups)
    n, many, room = len(groups), len(couplings), held.shape[1] // EDGE
    wide = -(-n * 4 * modes // EDGE) * EDGE
    tall = -(-modes // 8) * 8
    out = [jax.ShapeDtypeStruct((at.count, tall, wide), held.dtype)] * many
    if spread:
        out = out[:-1] + [jax.ShapeDtypeStruct((tall, wide), held.dtype)] * at.count
    me = lax.axis_index("sub").astype(jnp.int32)[None]
    return pl.pallas_call(
        functools.partial(project_kernel, at, room, sets, many, spread),
        out_shape=out,
        in_specs=[pl.BlockSpec(memory_space=pltpu.SMEM)] * 2
        + [pl.BlockSpec(memory_space=pltpu.HBM)] * (many + len(flat)),
        out_specs=[pl.BlockSpec(memory_space=pltpu.VMEM)] * len(out),
        scratch_shapes=[pltpu.VMEM(held.shape, held.dtype)] * many
        + [pltpu.VMEM((at.count + 1, 4 * ROWS, n * EDGE), jnp.float32)] * many
        + [
            pltpu.VMEM((len(flat), modes, held.shape[1]), held.dtype),
            pltpu.VMEM((n * EDGE, BITE * EDGE), held.dtype),
            pltpu.SemaphoreType.DMA((2 * many,)),
            pltpu.SemaphoreType.DMA((len(flat),)),
        ],
        compiler_params=pltpu.CompilerParams(vmem_limit_bytes=56 * MIB),
        cost_estimate=LIGHT,
    )(meta, me, *couplings, *flat)


def couple_end(at, meta, ints, places, phi_in, blocks):
    live, _, col = ints
    phis = [one[None] for one in phi_in]
    return couple(at, ROOM, meta, live, places, col, phis, *blocks, cost=HEAVY)


def assemble_kernel(modes, place, near, second, *refs):
    rows = refs[-2].shape[1]
    thirds, (grid_k, grid_m, wide, sorted_third) = refs[:-4], refs[-4:]
    third = thirds[0]
    if len(thirds) > 1:
        third = sorted_third
        for k, one in enumerate(thirds):
            third[jnp.bitwise_xor(place[1], k)] = one[...]
    own, left, right = ((near, g * 4 * modes) for g in range(3))
    second, third = (second, 0), (third, 0)
    plans = (
        (own, right, second, third),
        (left, own, right, second),
        (second, left, own, right),
        (third, second, left, own),
    )
    for which, grid in enumerate((grid_k, grid_m)):
        for z, plan in enumerate(plans):

            @pl.when(place[0] == z)
            def _(plan=plan, which=which):
                for far in range(2):
                    for h, (part, base) in enumerate(plan):
                        take = base + (2 * which + far) * modes
                        at = (4 * far + h) * modes
                        wide[:, :, at : at + modes] = part[:, :rows, take : take + modes].astype(
                            jnp.float32
                        )

        grid[...] = jnp.transpose(wide[...], (1, 0, 2))


def assemble(place, parts, thirds, modes, rows):
    owners = parts[0].shape[0]
    out = jax.ShapeDtypeStruct((rows, owners, 8 * modes), jnp.float32)
    group = min(owners, 8)
    block = pl.BlockSpec((rows, group, 8 * modes), lambda d, place: (0, d, 0))

    def taken(part):
        if len(part.shape) == 2:
            return pl.BlockSpec(part.shape, lambda d, place: (0, 0))
        return pl.BlockSpec((group, *part.shape[1:]), lambda d, place: (d, 0, 0))

    return pl.pallas_call(
        functools.partial(assemble_kernel, modes),
        out_shape=[out, out],
        grid_spec=pltpu.PrefetchScalarGridSpec(
            num_scalar_prefetch=1,
            grid=(owners // group,),
            in_specs=[taken(part) for part in (*parts, *thirds)],
            out_specs=[block] * 2,
            scratch_shapes=[
                pltpu.VMEM((group, rows, 8 * modes), jnp.float32),
                pltpu.VMEM((group, *thirds[0].shape[-2:]), thirds[0].dtype),
            ],
        ),
        compiler_params=pltpu.CompilerParams(vmem_limit_bytes=56 * MIB),
        cost_estimate=LIGHT,
    )(place, *parts, *thirds)


def moved(shard, axis, by, sources=None):
    length = lax.axis_size(axis)
    sources = range(length) if sources is None else sources
    pairs = [(i, i + by) for i in sources if 0 <= i + by < length]
    return lax.ppermute(shard, axis, pairs)


def to_owners(part, modes):
    count, _, cols = part.shape
    owners = lax.axis_size("sub")
    if owners != count:
        part = part[:, :modes].reshape(owners, count * modes // owners, cols)
    return lax.all_to_all(part, "sub", split_axis=0, concat_axis=0, tiled=True)


def sent_in(phi_packed):
    last = lax.axis_size("grp") - 1
    return moved(phi_packed, "grp", 1, [0]), moved(phi_packed, "grp", -1, [last])


def sent_back(part):
    last = lax.axis_size("grp") - 1
    return lax.ppermute(part, "grp", [(1, 0), (last - 1, last)])


def sent_to_owners(parts):
    last, owners = lax.axis_size("grp") - 1, lax.axis_size("sub")
    moved_to = []
    for k, part in enumerate(parts):
        pairs = []
        for source, target in ((1, 0), (last - 1, last)):
            for sub in range(owners):
                pairs.append((sub * (last + 1) + source, (sub ^ k) * (last + 1) + target))
        moved_to.append(lax.ppermute(part, ("sub", "grp"), pairs))
    return moved_to


def both_ways(left, right):
    return moved(left, "grp", 1), moved(right, "grp", -1)


def main_path(at, lists, ints, phi, psi, border, blocks):
    meta, phi_meta, places, beside = lists
    modes = phi.shape[1]
    hold = lax.optimization_barrier

    own = pack(at, 0, ROOM, meta, psi, border)
    one = both_ways(own, own)
    own, phi, phi_meta = hold((own, phi, phi_meta))
    coupling = couple(at, ROOM, meta, *ints, [phi], *blocks)
    phi_in = sent_in(pack(at, 0, PHI_ROOM, phi_meta, phi))
    one, coupling, beside = hold((one, coupling, beside))
    last = lax.axis_size("grp") - 1
    two = (
        moved(one[0], "grp", 1, range(1, last)),
        moved(one[1], "grp", -1, range(last - 1, 0, -1)),
    )
    (near,) = project(at, meta, [coupling], [(own,), (one[0],), (one[1],)])
    near = to_owners(near, modes)
    end = couple_end(at, meta, ints, places, phi_in, blocks)
    two, near, end = hold((two, near, end))
    direct = lax.axis_size("sub") == phi.shape[0]
    second, *third = project(at, meta, [coupling, end], [two], spread=direct)
    third = sent_to_owners(third) if direct else [sent_back(third[0])]
    second = to_owners(second, modes)
    if not direct:
        third, second, near = hold((third, second, near))
        third = [to_owners(third[0], modes)]
    place = jnp.stack([lax.axis_index("grp"), lax.axis_index("sub")]).astype(jnp.int32)
    rows = phi.shape[0] * modes // lax.axis_size("sub")
    return assemble(place, (near, second), third, modes, rows), two, beside, phi


def without(at, meta, by, room):
    kept = jnp.concatenate([meta[: at.start], jnp.full((at.start,), at.blocks_per, jnp.int32)])
    order = lax.dynamic_slice_in_dim(kept, by, at.start, 0)
    return jnp.concatenate([order, jnp.clip(meta[at.start :] - by, 0, room)])


def columns(part, modes, rows, groups):
    part = part[:, :rows, : groups * 4 * modes].astype(jnp.float32)
    part = part.reshape(*part.shape[:2], groups, 2, 2, modes).transpose(3, 1, 0, 4, 2, 5)
    return part.reshape(2, *part.shape[1:3], 2 * groups * modes)


def add_kernel(old, new, out):
    out[...] = old[...] + new[...]


def added(old, new):
    rows, owners, cols = old.shape
    block = pl.BlockSpec((rows, min(owners, 8), cols), lambda d: (0, d, 0))
    return pl.pallas_call(
        add_kernel,
        out_shape=jax.ShapeDtypeStruct(old.shape, old.dtype),
        grid=(owners // min(owners, 8),),
        in_specs=[block, block],
        out_specs=block,
        input_output_aliases={0: 0},
        compiler_params=pltpu.CompilerParams(vmem_limit_bytes=32 * MIB),
    )(old, new)


def per_device(phi, psi, k_blocks, m_blocks, block_row, block_col, live):
    count, modes, width = phi.shape
    at = Meta(count, k_blocks.shape[1], width // EDGE)
    blocks = (k_blocks, m_blocks)
    ints = (live, block_row, block_col)
    border = moved(psi[count - 1], "sub", 1)
    (whole,) = listed(at, 0, block_col, live)
    phi_whole, places = listed(at, 1, block_row, live, with_places=True)
    total = at.start + count + 1
    most = lax.pmax(jnp.stack([whole[total], phi_whole[total]]), "sub")
    over = jnp.maximum(most - jnp.asarray([ROOM, PHI_ROOM], jnp.int32), 0)
    each = jnp.asarray([MORE, PHI_ROOM], jnp.int32)
    trips = jnp.max((over + each - 1) // each)
    meta = jnp.concatenate([whole[: at.start], jnp.minimum(whole[at.start :], ROOM)])
    lists = (meta, phi_whole, places, trips)
    grids, far, trips, phi = main_path(at, lists, ints, phi, psi, border, blocks)

    def turned(whole):
        return whole.transpose(1, 0, 2)

    def more(state):
        n, phi, psi, far, before = state[0], state[1], state[2], state[3], state[4:]
        phi, psi, far = lax.optimization_barrier((phi, psi, far))
        phi, psi = turned(phi), turned(psi)

        rest = without(at, whole, ROOM + n * MORE, MORE)
        packed = pack(at, 0, MORE, rest, psi, border)
        packed = jnp.stack([packed] * lax.axis_size("grp"))
        packed = lax.all_to_all(packed, "grp", split_axis=0, concat_axis=0, tiled=True)
        coupling = couple(at, MORE, rest, *ints, [phi], *blocks)
        shards = [(packed[h],) for h in range(packed.shape[0])]
        part = to_owners(project(at, rest, [coupling], shards)[0], modes)
        after = columns(part, modes, grids[0].shape[0], len(shards))

        skipped = (n + 1) * PHI_ROOM
        rest = without(at, phi_whole, skipped, PHI_ROOM)
        phi_in = sent_in(pack(at, 0, PHI_ROOM, rest, phi))
        end = couple_end(at, meta, ints, places - skipped, phi_in, blocks)
        (part,) = project(at, meta, [end], [far])
        part = columns(to_owners(sent_back(part), modes), modes, grids[0].shape[0], 1)
        place, zero = lax.axis_index("grp"), jnp.zeros_like(part[..., :modes])
        last = lax.axis_size("grp") - 1
        ends = []
        for low in (0, modes):
            one = part[..., low : low + modes]
            for h in range(last + 1):
                wanted = ((place == 0) & (h == last)) | ((place == last) & (h == 0))
                ends.append(jnp.where(wanted, one, zero))
        after = after + jnp.concatenate(ends, axis=-1)
        return (n + 1, *state[1:4], *(added(old, new) for old, new in zip(before, after)))

    state = (jnp.int32(0), turned(phi), turned(psi), far, *grids)
    state = lax.while_loop(lambda state: state[0] < trips, more, state)
    return tuple(turned(grid)[None, None] for grid in state[4:])


def solution(mesh):
    placed = (
        P("sub", "grp", None),
        P("sub", "grp", None),
        P("sub", None, None, None),
        P("sub", None, None, None),
        P("sub", None),
        P("sub", None),
        P("sub"),
    )
    return jax.shard_map(
        per_device,
        mesh=mesh,
        in_specs=placed,
        out_specs=(P("sub", "grp", None, None, None), P("sub", "grp", None, None, None)),
        check_vma=False,
    )
```
